128 devices in a mesh: ctx: 32 (over z, x, y_lo), head: 4 (over y_hi, core).
Axes of the slice: x: 4, y: 4 (y_hi: 2, y_lo: 2; y = y_hi * 2 + y_lo), z: 4, core: 2. Of those that a mesh axis runs over, the one named last changes fastest.
Arguments:
- queries: bfloat16 [49152, 1024], P(('ctx', 'head')), may hold values from -24 to 24
- keys: bfloat16 [49152, 1024], P(('ctx', 'head')), may hold values from -24 to 24
- values: bfloat16 [49152, 1024], P(('ctx', 'head')), may hold values from -6 to 6
- grad_out: bfloat16 [49152, 1024], P(('ctx', 'head')), may hold values from -6 to 6
- offset_mid: int32 [16], P('head'), may hold values from 0 to 3
- head_top_offsets: int32 [16], P('head'), may hold values from 0 to 31
Outputs:
- attended: bfloat16 [49152, 1024], P(('ctx', 'head'))
- grad_queries: bfloat16 [49152, 1024], P(('ctx', 'head'))
- grad_keys: bfloat16 [49152, 1024], P(('ctx', 'head'))
- grad_values: bfloat16 [49152, 1024], P(('ctx', 'head'))
The draws below stay inside these ranges and needn't reach their ends.
All inputs are finite; a program needn't handle non-finite values.
Results may differ from the reference program's by a relative error of at most 0.009.
Values may be sent and summed in bfloat16 or wider, within the bound.
A program may use at most 128 MiB of HBM per device.

```python
import math
import jax
import jax.numpy as jnp
from jax import lax

HEAD_COUNT = 16
HD = 64
TOKENS_PER_SHARD = 1536
MIDDLE_DILATION = 4
TOP_DILATION = 32
TOKENS = 49152


def draw_queries(key, part):
    key = jax.random.fold_in(key, 11)
    own_rows = jnp.clip(jax.random.normal(key, (TOKENS, HEAD_COUNT * HD), jnp.float32), -4.0, 4.0)
    return own_rows.astype(jnp.bfloat16)


def draw_keys(key, part):
    key = jax.random.fold_in(key, 12)
    own_rows = jnp.clip(jax.random.normal(key, (TOKENS, HEAD_COUNT * HD), jnp.float32), -4.0, 4.0)
    return own_rows.astype(jnp.bfloat16)


def draw_offset_mid(key, part):
    key = jax.random.fold_in(key, 21)
    return jax.random.randint(key, (HEAD_COUNT,), 0, MIDDLE_DILATION, dtype=jnp.int32)


def set_ends(drawn, key, low, top_value):
    dims = drawn.shape
    spot = [jax.random.randint(jax.random.fold_in(key, axis), (), 0, dims[axis]) for axis in range(len(dims))]
    drawn = drawn.at[tuple(spot)].set(low)
    longest = dims.index(max(dims))
    spot[longest] = (spot[longest] + 1) % dims[longest]
    return drawn.at[tuple(spot)].set(top_value)


def block_levels(key, extent, shards, smallest, high):
    def one(dim, parts):
        steps = jax.random.uniform(jax.random.fold_in(jax.random.fold_in(key, 6), dim), (parts,), jnp.float32, smallest / len(shards), high / len(shards))
        return jnp.repeat(jnp.exp(steps), extent[dim] // parts).reshape((-1,) + (1,) * (len(extent) - dim - 1))

    gain = one(*shards[0])
    for cut in shards[1:]:
        gain = gain * one(*cut)
    return gain


def centred(own_key, dims, deviation, reach, shards=(), held_as=jnp.bfloat16):
    values = deviation * jax.random.normal(own_key, dims, jnp.float32)
    if shards:
        values = values * block_levels(own_key, dims, shards, -0.22, 0.18)
    return jnp.clip(values, -reach, reach).astype(held_as)


def setup_inputs(seed: int = 0) -> dict:
    key_of = jax.random.split(jax.random.key(seed), 7)
    return {
        "queries": draw_queries(jax.random.fold_in(key_of[6], 71), 0),
        "keys": draw_keys(jax.random.fold_in(key_of[6], 71), 0),
        "values": centred(key_of[2], (TOKENS, HEAD_COUNT * HD), 1.0, 6.0, ((0, 128),)),
        "grad_out": centred(key_of[3], (TOKENS, HEAD_COUNT * HD), 1.0, 6.0, ((0, 128),)),
        "offset_mid": draw_offset_mid(jax.random.fold_in(key_of[6], 71), 0),
        "head_top_offsets": set_ends(jax.random.randint(key_of[5], (HEAD_COUNT,), 0, TOP_DILATION), jax.random.fold_in(key_of[5], 1), 0, TOP_DILATION - 1).astype(jnp.int32),
    }


NEGATIVE = -1e30


def block_scores(query_block, query_order, key_head, key_order, score_scale):
    scores = lax.dot_general(query_block, key_head, (((1,), (1,)), ((), ())), preferred_element_type=jnp.float32) * score_scale
    allowed = key_order[None, :] <= query_order[:, None]
    return jnp.where(allowed, scores, NEGATIVE), allowed


def block_forward(query_block, query_order, key_head, value_head, key_order, score_scale):
    scores, allowed = block_scores(query_block, query_order, key_head, key_order, score_scale)
    row_max = jnp.max(scores, axis=1)
    weights = jnp.exp(scores - row_max[:, None])
    row_total = jnp.sum(weights, axis=1)
    mixed_rows = jnp.dot(weights.astype(jnp.bfloat16), value_head, preferred_element_type=jnp.float32) / row_total[:, None]
    return mixed_rows, row_max + jnp.log(row_total)


def block_backward(query_block, query_order, key_head, value_head, key_order, log_total, share_rows, out_dot, grad_block, score_scale):
    scores, allowed = block_scores(query_block, query_order, key_head, key_order, score_scale)
    probs = jnp.where(allowed, jnp.exp(scores - log_total[:, None]), 0.0)
    weighted = share_rows[:, None] * probs
    dprob = lax.dot_general(grad_block, value_head, (((1,), (1,)), ((), ())), preferred_element_type=jnp.float32)
    dscore = (weighted * (dprob - out_dot[:, None]) * score_scale).astype(jnp.bfloat16)
    d_query = jnp.dot(dscore, key_head, preferred_element_type=jnp.float32)
    d_key = lax.dot_general(dscore, query_block, (((0,), (0,)), ((), ())), preferred_element_type=jnp.float32)
    d_value = lax.dot_general(weighted.astype(jnp.bfloat16), grad_block, (((0,), (0,)), ((), ())), preferred_element_type=jnp.float32)
    return d_query, d_key, d_value


def level_forward(queries_h, query_order, keys_h, values_h, key_order):
    n_query = queries_h.shape[1]
    block_rows = math.gcd(n_query, 512)
    block_count = n_query // block_rows
    score_scale = queries_h.shape[2] ** -0.5

    def one_head(head_item):
        q_head, k_head, v_head = head_item

        def one_block(block_part):
            return block_forward(block_part[0], block_part[1], k_head, v_head, key_order, score_scale)

        mixed_rows, log_total = lax.map(one_block, (q_head.reshape(block_count, block_rows, -1), query_order.reshape(block_count, block_rows)))
        return mixed_rows.reshape(n_query, -1), log_total.reshape(n_query)

    return lax.map(one_head, (queries_h, keys_h, values_h))


def level_backward(queries_h, query_order, keys_h, values_h, key_order, log_total, share_rows, out_dot, grads_h, want_query, want_keys):
    n_query = queries_h.shape[1]
    block_rows = math.gcd(n_query, 512)
    block_count = n_query // block_rows
    score_scale = queries_h.shape[2] ** -0.5

    def one_head(head_item):
        q_head, k_head, v_head, l_head, s_head, o_head, g_head = head_item
        blocks = (q_head.reshape(block_count, block_rows, -1), query_order.reshape(block_count, block_rows), l_head.reshape(block_count, block_rows), s_head.reshape(block_count, block_rows), o_head.reshape(block_count, block_rows), g_head.reshape(block_count, block_rows, -1))
        zero_keys = jnp.zeros(k_head.shape, jnp.float32)

        def step(key_sums, block_part):
            d_query, d_key, d_value = block_backward(block_part[0], block_part[1], k_head, v_head, key_order, block_part[2], block_part[3], block_part[4], block_part[5], score_scale)
            if want_keys:
                key_sums = (key_sums[0] + d_key, key_sums[1] + d_value)
            if want_query:
                return key_sums, d_query
            return key_sums, jnp.zeros((1,), jnp.float32)

        key_sums, d_queries = lax.scan(step, (zero_keys, zero_keys), blocks)
        if want_query:
            d_queries = d_queries.reshape(n_query, -1)
        return d_queries, key_sums[0], key_sums[1]

    return lax.map(one_head, (queries_h, keys_h, values_h, log_total, share_rows, out_dot, grads_h))


def reference(queries, keys, values, grad_out, offset_mid, head_top_offsets):
    def head_major(array):
        return array.reshape(TOKENS, HEAD_COUNT, HD).transpose(1, 0, 2)

    order_rows = jnp.arange(TOKENS_PER_SHARD, dtype=jnp.int32)

    def pick(array, dilation, offset):
        shaped = array.reshape((TOKENS // dilation, dilation) + array.shape[1:])
        return lax.dynamic_index_in_dim(shaped, offset, 1, keepdims=False)

    def place(array, dilation, offset):
        selected = jnp.arange(dilation, dtype=jnp.int32) == offset
        selected = selected.reshape((1, dilation) + (1,) * (array.ndim - 1))
        spread = jnp.where(selected, array[:, None], jnp.zeros((), array.dtype))
        return spread.reshape((TOKENS,) + array.shape[1:])

    def segments(array):
        return array.reshape((-1, TOKENS_PER_SHARD) + array.shape[1:])

    def one_head(head_item):
        q_head, k_head, v_head, g_head, middle_row_shift, top_row_shift = head_item
        level_layout = ((1, jnp.zeros((), jnp.int32)), (MIDDLE_DILATION, middle_row_shift), (TOP_DILATION, top_row_shift))
        level_outs = []
        level_totals = []
        full_totals = []
        for dilation, offset in level_layout:
            mixed_rows, log_total = level_forward(segments(pick(q_head, dilation, offset)), order_rows, segments(pick(k_head, dilation, offset)), segments(pick(v_head, dilation, offset)), order_rows)
            level_outs.append(place(mixed_rows.reshape(-1, HD), dilation, offset))
            log_total = log_total.reshape(-1)
            level_totals.append(log_total)
            used = place(jnp.ones((TOKENS // dilation,), jnp.float32), dilation, offset) > 0.5
            full_totals.append(jnp.where(used, place(log_total, dilation, offset), NEGATIVE))
        peak_value = jnp.maximum(jnp.maximum(full_totals[0], full_totals[1]), full_totals[2])
        level_terms = [jnp.exp(total_row - peak_value) for total_row in full_totals]
        norm_sum = level_terms[0] + level_terms[1] + level_terms[2]
        shares = [term_row / norm_sum for term_row in level_terms]
        mixed = shares[0][:, None] * level_outs[0] + shares[1][:, None] * level_outs[1] + shares[2][:, None] * level_outs[2]
        out_dot = jnp.sum(g_head.astype(jnp.float32) * mixed, axis=1)
        d_queries = jnp.zeros((TOKENS, HD), jnp.float32)
        d_keys = jnp.zeros((TOKENS, HD), jnp.float32)
        d_values = jnp.zeros((TOKENS, HD), jnp.float32)
        for level_number, (dilation, offset) in enumerate(level_layout):
            d_query, d_key, d_value = level_backward(segments(pick(q_head, dilation, offset)), order_rows, segments(pick(k_head, dilation, offset)), segments(pick(v_head, dilation, offset)), order_rows, segments(level_totals[level_number]), segments(pick(shares[level_number], dilation, offset)), segments(pick(out_dot, dilation, offset)), segments(pick(g_head, dilation, offset)), True, True)
            d_queries = d_queries + place(d_query.reshape(-1, HD), dilation, offset)
            d_keys = d_keys + place(d_key.reshape(-1, HD), dilation, offset)
            d_values = d_values + place(d_value.reshape(-1, HD), dilation, offset)
        return mixed.astype(jnp.bfloat16), d_queries.astype(jnp.bfloat16), d_keys.astype(jnp.bfloat16), d_values.astype(jnp.bfloat16)

    results = lax.map(one_head, (head_major(queries), head_major(keys), head_major(values), head_major(grad_out), offset_mid, head_top_offsets))

    def token_major(array):
        return array.transpose(1, 0, 2).reshape(TOKENS, HEAD_COUNT * HD)

    return token_major(results[0]), token_major(results[1]), token_major(results[2]), token_major(results[3])
```

```python
import functools

import jax
import jax.numpy as jnp
from jax import lax
from jax.experimental import pallas as pl
from jax.experimental.pallas import tpu as pltpu
from jax.sharding import PartitionSpec as P

MESH = pl.DeviceIdType.MESH
HD = 64
MIDDLE = 4
B = 256
NEG = -1e30
F32 = jnp.float32
BF = jnp.bfloat16
Q, K, V, G = 0, 1, 2, 3


def dot(a, b):
    return jnp.dot(a, b, preferred_element_type=F32)


def iota(shape, dim):
    return lax.broadcasted_iota(jnp.int32, shape, dim)


def keep(x, mask):
    return jnp.where(mask, x, jnp.zeros_like(x))


def half_rows(x, e):
    return keep(x, (iota(x.shape, 0) >= HD) == (e == 1))


def half_lanes(x, e):
    return keep(x, (iota(x.shape, 1) >= HD) == (e == 1))


def split3(x):
    hi = x.astype(BF).astype(F32)
    rest = x - hi
    mid = rest.astype(BF).astype(F32)
    return hi, mid, rest - mid


def stack_rows(rows, count):
    n = rows[0].shape[1]
    at = iota((count, n), 0)
    out = jnp.zeros((count, n), F32)
    for i, row in enumerate(rows):
        out = jnp.where(at == i, row, out)
    return out.astype(BF)


def quarter(at, step):
    return (
        (at >= step).astype(jnp.int32)
        + (at >= 2 * step).astype(jnp.int32)
        + (at >= 3 * step).astype(jnp.int32)
    )


def kernel(
    C, H, T,
    offm, offt, q_in, k_in, v_in, g_in,
    o_out, dq_out, dk_out, dv_out,
    xin, xt, pst, mkv, mkt, mqt, pmid, smid, tkv, tkt, tbd, tbdt, ptop,
    e2, e2t, et, ett, o1, omt, ott, st1, stm, stt, cd1, cdm, cdt,
    dqt, dk, dv, dqmt, dqtt, mout, mrec, tout, trec, ostage,
    in_s, in_r, in_l, ms, mr, mps, mpr, ts, tr, tps, tpr, os_, or_, ol,
):
    R = T * H
    NB = R // B
    MC = R // MIDDLE
    TC = R // C
    TQ = 4 * TC
    NJ = MC // 128
    c = lax.axis_index("ctx")
    h = lax.axis_index("head")
    d = lax.rem(c, MIDDLE)
    ins = (q_in, k_in, v_in, g_in)
    outs = (o_out, dq_out, dk_out, dv_out)

    bar = pltpu.get_barrier_semaphore()
    for s in range(1, H):
        pl.semaphore_signal(bar, inc=1, device_id=(c, lax.rem(h + s, H)), device_id_type=MESH)

    def greet(s, carry):
        pl.semaphore_signal(bar, inc=1, device_id=(lax.rem(c + s, C), h), device_id_type=MESH)
        return carry

    lax.fori_loop(1, C, greet, 0)
    pl.semaphore_wait(bar, H - 1 + C - 1)

    def remote(src, dst, ssem, rsem, dev):
        return pltpu.make_async_remote_copy(
            src_ref=src, dst_ref=dst, send_sem=ssem, recv_sem=rsem,
            device_id=dev, device_id_type=MESH,
        )

    def lanes(head, p):
        return pl.ds(pl.multiple_of(head * 256 + p * 128, 128), 128)

    def in_copy(a, p, s):
        to = lax.rem(h + s, H)
        i = (a * 2 + p) * 3 + s - 1
        return remote(
            ins[a].at[:, lanes(to, p)], xin.at[a, p, pl.ds(h * T, T)],
            in_s.at[i], in_r.at[i], (c, to),
        )

    def in_local(a, p):
        return pltpu.make_async_copy(
            ins[a].at[:, lanes(h, p)], xin.at[a, p, pl.ds(h * T, T)], in_l.at[a * 2 + p]
        )

    for a, p in ((K, 0), (Q, 0), (V, 0), (K, 1), (V, 1), (Q, 1), (G, 0), (G, 1)):
        for s in (2, 1, 3):
            in_copy(a, p, s).start()
        in_local(a, p).start()

    def in_wait(a, p):
        in_local(a, p).wait()
        for s in (1, 2, 3):
            in_copy(a, p, s).wait()

    for p in (0, 1):
        r = iota((256, 512), 0)
        odd = r >= 128
        e2[p] = (
            iota((256, 512), 1)
            == 4 * (r - jnp.where(odd, 128, 0)) + jnp.where(odd, offm[2 * p + 1], offm[2 * p])
        ).astype(F32).astype(BF)
        r = iota((512, 256), 1)
        odd = r >= 128
        e2t[p] = (
            iota((512, 256), 0)
            == 4 * (r - jnp.where(odd, 128, 0)) + jnp.where(odd, offm[2 * p + 1], offm[2 * p])
        ).astype(F32).astype(BF)

    def top_hot(shape, dim):
        r = iota(shape, dim)
        n = quarter(r, TC)
        off = jnp.where(
            n < 2, jnp.where(n == 0, offt[0], offt[1]), jnp.where(n == 2, offt[2], offt[3])
        )
        return (iota(shape, 1 - dim) == C * (r - TC * n) + off).astype(F32).astype(BF)

    et[...] = top_hot((TQ, R), 0)
    ett[...] = top_hot((R, TQ), 1)

    row_head = quarter(iota((TQ, 128), 0), TC)
    lane_odd = (iota((TQ, 128), 1) >= HD).astype(jnp.int32)

    def arrived(a, p):
        in_wait(a, p)
        x = xin[a, p]
        xt[a, p] = (x * 0.125).T if a == Q else x.T
        low = iota((128, 128), 1) < HD
        for j in range(NJ):
            r = dot(e2[p], xin[a, p, j * 512 : (j + 1) * 512])
            picked = jnp.where(low, r[:128], r[128:]).astype(BF)
            if a in (K, V):
                mkv[d, a - K, p, j * 128 : (j + 1) * 128] = picked
            else:
                if a == Q:
                    picked = picked * 0.125
                mqt[0 if a == Q else 1, p, :, j * 128 : (j + 1) * 128] = picked.T
        r = dot(et[...], xin[a, p])
        if a in (K, V):
            low = iota((TC, 128), 1) < HD
            picked = jnp.where(low, r[2 * p * TC : (2 * p + 1) * TC], r[(2 * p + 1) * TC : (2 * p + 2) * TC])
            tkv[c, a - K, :, p * 128 : (p + 1) * 128] = picked.astype(BF)
        else:
            if a == Q:
                r = r * 0.125
            r = keep(r, row_head == 2 * p + lane_odd)
            tbd[0 if a == Q else 1, :, p * 128 : (p + 1) * 128] = r.astype(BF)

    def where_p(kb, i):
        if kb < NB // 2:
            return kb * B, (i - kb) * B
        return (NB - 1 - kb) * B, (i + 1) * B

    def p_block(n, kb, i):
        r, l = where_p(kb, i)
        return pst.at[n, r : r + B, l : l + B]

    def p_tail(n, kb):
        r, l = where_p(kb, kb)
        return pst[n, r : r + B, l : l + (NB - kb) * B]

    def forward_one(p):
        causal = iota((B, B), 0) <= iota((B, B), 1)
        for i in range(NB):
            n = (i + 1) * B
            for e in (0, 1):
                hh = 2 * p + e
                s = dot(xin[K, p, :n], half_rows(xt[Q, p, :, i * B : n], e))
                sd = jnp.where(causal, s[n - B :], NEG)
                m = jnp.max(sd, axis=0, keepdims=True)
                if i:
                    m = jnp.maximum(m, jnp.max(s[: n - B], axis=0, keepdims=True))
                total = None
                parts = []
                for kb in range(i + 1):
                    w = jnp.exp((sd if kb == i else s[kb * B : (kb + 1) * B]) - m)
                    t = jnp.sum(w, axis=0, keepdims=True)
                    total = t if total is None else total + t
                    w = w.astype(BF)
                    p_block(hh, kb, i)[...] = w
                    parts.append(w)
                w = parts[0] if i == 0 else jnp.concatenate(parts, axis=0)
                o1[hh * HD : (hh + 1) * HD, i * B : n] = dot(xt[V, p, e * HD : (e + 1) * HD, :n], w)
                st1[hh : hh + 1, i * B : n] = m
                st1[4 + hh : 5 + hh, i * B : n] = total

    for a in (K, Q, V):
        arrived(a, 0)
    forward_one(0)
    for a in (K, V):
        arrived(a, 1)

    base = c - d

    def mid_send(s):
        return remote(mkv.at[d], mkv.at[d], ms.at[s - 1], mr.at[s - 1], (lax.rem(base + d + s, C), h))

    def mid_recv(s):
        frm = lax.rem(d + MIDDLE - s, MIDDLE)
        return remote(mkv.at[frm], mkv.at[frm], ms.at[s - 1], mr.at[s - 1], (lax.rem(base + d + s, C), h))

    for s in range(1, MIDDLE):
        @pl.when(d + s < MIDDLE)
        def _():
            mid_send(s).start()

    def top_copy(s):
        return remote(tkv.at[c], tkv.at[c], ts.at[s], tr.at[s], (lax.rem(c + s, C), h))

    def top_arrival(s):
        frm = lax.rem(c + C - s, C)
        return remote(tkv.at[frm], tkv.at[frm], ts.at[s], tr.at[s], (lax.rem(c + s, C), h))

    def start_top(s, carry):
        top_copy(s).start()
        return carry

    lax.fori_loop(1, C, start_top, 0)

    arrived(Q, 1)
    forward_one(1)
    for p in (0, 1):
        arrived(G, p)
    tbdt[0] = tbd[0].T
    tbdt[1] = tbd[1].T

    def wait_top(s, carry):
        top_copy(s).wait_send()
        top_arrival(s).wait_recv()
        return carry

    lax.fori_loop(1, C, wait_top, 0)
    col = iota((1, TQ), 1)
    col_head = quarter(col, TC)
    diag = quarter(iota((256, TQ), 0), HD) == col_head
    tk = tkv[:, 0].reshape(R, 256)
    tv = tkv[:, 1].reshape(R, 256)
    tkt[0] = tk.T
    tkt[1] = tv.T
    s = dot(tk, tbdt[0])
    s = jnp.where(iota((R, TQ), 0) <= c * TC + col - TC * col_head, s, NEG)
    m = jnp.max(s, axis=0, keepdims=True)
    w = jnp.exp(s - m)
    total = jnp.sum(w, axis=0, keepdims=True)
    w = w.astype(BF)
    ptop[...] = w
    ott[...] = keep(dot(tkt[1], w), diag) / total
    stt[0:1] = m
    stt[1:2] = total

    for s in range(1, MIDDLE):
        @pl.when(d + s < MIDDLE)
        def _():
            mid_send(s).wait_send()

        @pl.when(d >= s)
        def _():
            mid_recv(s).wait_recv()

    def turn(kb, carry):
        for a in (0, 1):
            for p in (0, 1):
                mkt[kb, a, p] = mkv[kb, a, p].T
        return carry

    lax.fori_loop(0, d + 1, turn, 0)
    causal_mid = iota((MC, MC), 0) <= iota((MC, MC), 1)
    for p in (0, 1):
        for e in (0, 1):
            hh = 2 * p + e
            s = jnp.where(causal_mid, dot(mkv[d, 0, p], half_rows(mqt[0, p], e)), NEG)
            smid[e, d] = s
            stm[hh : hh + 1] = jnp.max(s, axis=0, keepdims=True)

        def scores(kb, carry):
            for e in (0, 1):
                hh = 2 * p + e
                s = dot(mkv[kb, 0, p], half_rows(mqt[0, p], e))
                smid[e, kb] = s
                stm[hh : hh + 1] = jnp.maximum(stm[hh : hh + 1], jnp.max(s, axis=0, keepdims=True))
            return carry

        lax.fori_loop(0, d, scores, 0)
        for e in (0, 1):
            hh = 2 * p + e
            omt[hh * HD : (hh + 1) * HD] = jnp.zeros((HD, MC), F32)
            stm[4 + hh : 5 + hh] = jnp.zeros((1, MC), F32)

        def weigh(kb, carry):
            for e in (0, 1):
                hh = 2 * p + e
                w = jnp.exp(smid[e, kb] - stm[hh : hh + 1])
                stm[4 + hh : 5 + hh] += jnp.sum(w, axis=0, keepdims=True)
                w = w.astype(BF)
                pmid[hh, kb] = w
                omt[hh * HD : (hh + 1) * HD] += dot(mkt[kb, 1, p, e * HD : (e + 1) * HD], w)
            return carry

        lax.fori_loop(0, d + 1, weigh, 0)

    token = iota((1, R), 1)

    def spread_mid(x, hh):
        p, e = hh // 2, hh % 2
        hot = e2[p, e * 128 : (e + 1) * 128]
        return jnp.concatenate([dot(x[:, j * 128 : (j + 1) * 128], hot) for j in range(NJ)], axis=1)

    def high_low(x):
        hi = x.astype(BF)
        return hi, (x - hi.astype(F32)).astype(BF)

    t_log = stt[0:1] + jnp.log(stt[1:2])
    cdt[...] = jnp.zeros_like(cdt)
    for hh in range(4):
        p, e = hh // 2, hh % 2
        rows = slice(hh * HD, (hh + 1) * HD)
        m_total = stm[4 + hh : 5 + hh]
        m_log = stm[hh : hh + 1] + jnp.log(m_total)
        hi, lo = high_low(omt[rows] / m_total)
        spread = spread_mid(jnp.concatenate([hi, lo, stack_rows(split3(m_log), 16)], axis=0), hh)
        out_m = spread[:HD] + spread[HD : 2 * HD]
        log_m = spread[128:129] + spread[129:130] + spread[130:131]
        hi, lo = high_low(ott[rows])
        mine = jnp.where(col_head == hh, t_log, 0.0)
        spread = dot(jnp.concatenate([hi, lo, stack_rows(split3(mine), 16)], axis=0), et[...])
        out_t = spread[:HD] + spread[HD : 2 * HD]
        log_t = spread[128:129] + spread[129:130] + spread[130:131]
        log_m = jnp.where((token & (MIDDLE - 1)) == offm[hh], log_m, NEG)
        log_t = jnp.where((token & (C - 1)) == offt[hh], log_t, NEG)
        total = st1[4 + hh : 5 + hh]
        log_1 = st1[hh : hh + 1] + jnp.log(total)
        peak = jnp.maximum(jnp.maximum(log_1, log_m), log_t)
        e_1, e_m, e_t = jnp.exp(log_1 - peak), jnp.exp(log_m - peak), jnp.exp(log_t - peak)
        norm = e_1 + e_m + e_t
        s_1, s_m, s_t = e_1 / norm, e_m / norm, e_t / norm
        c_1 = s_1 / total
        mixed = c_1 * o1[rows] + s_m * out_m + s_t * out_t
        o1[rows] = mixed
        delta = jnp.sum(xt[G, p, e * HD : (e + 1) * HD].astype(F32) * mixed, axis=0, keepdims=True)
        cd1[hh : hh + 1] = c_1
        cd1[4 + hh : 5 + hh] = delta
        stats = stack_rows(split3(s_m) + split3(s_t) + split3(delta), 16)
        for j in range(NJ):
            g = dot(stats[:, j * 512 : (j + 1) * 512], e2t[p, :, e * 128 : (e + 1) * 128])
            at = slice(j * 128, (j + 1) * 128)
            cdm[hh : hh + 1, at] = (g[0:1] + g[1:2] + g[2:3]) / m_total[:, at]
            cdm[4 + hh : 5 + hh, at] = g[6:7] + g[7:8] + g[8:9]
        g = keep(dot(stats, ett[...]), col_head == hh)
        cdt[0:1] += g[3:4] + g[4:5] + g[5:6]
        cdt[1:2] += g[6:7] + g[7:8] + g[8:9]

    def out_copy(a, p, s):
        to = lax.rem(h + s, H)
        i = (a * 2 + p) * 3 + s - 1
        return remote(
            ostage.at[a, p, pl.ds(to * T, T)], outs[a].at[:, lanes(h, p)],
            os_.at[i], or_.at[i], (c, to),
        )

    def out_arrival(a, p, s):
        frm = lax.rem(h + H - s, H)
        i = (a * 2 + p) * 3 + s - 1
        return remote(
            ostage.at[a, p, pl.ds(h * T, T)], outs[a].at[:, lanes(frm, p)],
            os_.at[i], or_.at[i], (c, lax.rem(h + s, H)),
        )

    def out_local(a, p):
        return pltpu.make_async_copy(
            ostage.at[a, p, pl.ds(h * T, T)], outs[a].at[:, lanes(h, p)], ol.at[a * 2 + p]
        )

    def out_start(a, p):
        for s in (2, 1, 3):
            out_copy(a, p, s).start()
        out_local(a, p).start()

    for p in (0, 1):
        ostage[0, p] = o1[p * 128 : (p + 1) * 128].astype(BF).T
        out_start(0, p)

    t_c = cdt[0:1] / stt[1:2]
    dp = dot(tkv[:, 1].reshape(R, 256), tbdt[1])
    ds = (ptop[...].astype(F32) * (dp - cdt[1:2])).astype(BF)
    dqtt[...] = keep(dot(tkt[0], ds), diag) * (t_c * 0.125)
    gc = (tbdt[1].astype(F32) * t_c).astype(BF).T
    qc = (tbdt[0].astype(F32) * t_c).astype(BF).T
    tout[:, 0] = dot(ds, qc).astype(BF).reshape(C, TC, 256)
    tout[:, 1] = dot(ptop[...], gc).astype(BF).reshape(C, TC, 256)

    def part_copy(s):
        to = lax.rem(c + s, C)
        return remote(tout.at[to], trec.at[c], tps.at[s], tpr.at[s], (to, h))

    def part_arrival(s):
        frm = lax.rem(c + C - s, C)
        return remote(tout.at[frm], trec.at[frm], tps.at[s], tpr.at[s], (lax.rem(c + s, C), h))

    def start_part(s, carry):
        part_copy(s).start()
        return carry

    lax.fori_loop(1, C, start_part, 0)
    trec[c] = tout[c]

    for p in (0, 1):
        low = iota((128, MC), 0) < HD
        cm = jnp.where(low, cdm[2 * p : 2 * p + 1], cdm[2 * p + 1 : 2 * p + 2])
        gc = (mqt[1, p].astype(F32) * cm).astype(BF).T
        qc = (mqt[0, p].astype(F32) * cm).astype(BF).T
        dqmt[p * 128 : (p + 1) * 128] = jnp.zeros((128, MC), F32)

        def back(kb, carry):
            d_key = d_value = None
            for e in (0, 1):
                hh = 2 * p + e
                w = pmid[hh, kb]
                dp = dot(mkv[kb, 1, p], half_rows(mqt[1, p], e))
                ds = (w.astype(F32) * (dp - cdm[4 + hh : 5 + hh])).astype(BF)
                dqmt[hh * HD : (hh + 1) * HD] += dot(mkt[kb, 0, p, e * HD : (e + 1) * HD], ds)
                t = dot(w, half_lanes(gc, e))
                d_value = t if d_value is None else d_value + t
                t = dot(ds, half_lanes(qc, e))
                d_key = t if d_key is None else d_key + t
            mout[kb, 0, p] = d_key.astype(BF)
            mout[kb, 1, p] = d_value.astype(BF)
            return carry

        lax.fori_loop(0, d + 1, back, 0)
        dqmt[p * 128 : (p + 1) * 128] = dqmt[p * 128 : (p + 1) * 128] * (cm * 0.125)

    def mid_part(s):
        to = lax.rem(d + MIDDLE - s, MIDDLE)
        return remote(mout.at[to], mrec.at[s - 1], mps.at[s - 1], mpr.at[s - 1], (base + to, h))

    for s in range(1, MIDDLE):
        @pl.when(d >= s)
        def _():
            mid_part(s).start()

        @pl.when(d + s >= MIDDLE)
        def _():
            mrec[s - 1] = jnp.zeros(mrec.shape[1:], BF)

    def backward_one(p):
        low = iota((128, R), 0) < HD
        cm = jnp.where(low, cd1[2 * p : 2 * p + 1], cd1[2 * p + 1 : 2 * p + 2])
        gc = (xt[G, p].astype(F32) * cm).astype(BF).T
        qc = (xt[Q, p].astype(F32) * cm).astype(BF).T
        gcs = [half_lanes(gc, e) for e in (0, 1)]
        qcs = [half_lanes(qc, e) for e in (0, 1)]
        for kb in range(NB):
            dv[p, kb * B : (kb + 1) * B] = dot(p_tail(2 * p, kb), gcs[0][kb * B :]) + dot(
                p_tail(2 * p + 1, kb), gcs[1][kb * B :]
            )
        for i in range(NB):
            n = (i + 1) * B
            for e in (0, 1):
                hh = 2 * p + e
                dp = dot(xin[V, p, :n], half_rows(xt[G, p, :, i * B : n], e))
                delta = cd1[4 + hh : 5 + hh, i * B : n]
                parts = []
                for kb in range(i + 1):
                    w = p_block(hh, kb, i)[...].astype(F32)
                    ds = (w * (dp[kb * B : (kb + 1) * B] - delta)).astype(BF)
                    p_block(hh, kb, i)[...] = ds
                    parts.append(ds)
                ds = parts[0] if i == 0 else jnp.concatenate(parts, axis=0)
                dqt[hh * HD : (hh + 1) * HD, i * B : n] = dot(
                    xt[K, p, e * HD : (e + 1) * HD, :n], ds
                ) * (cd1[hh : hh + 1, i * B : n] * 0.125)
        for kb in range(NB):
            dk[p, kb * B : (kb + 1) * B] = dot(p_tail(2 * p, kb), qcs[0][kb * B :]) + dot(
                p_tail(2 * p + 1, kb), qcs[1][kb * B :]
            )

    def finish(p):
        x = keep(dqtt[p * 128 : (p + 1) * 128], diag[p * 128 : (p + 1) * 128]).astype(BF)
        grad = dqt[p * 128 : (p + 1) * 128] + dot(x, et[...])
        x = dqmt[p * 128 : (p + 1) * 128].astype(BF)
        grad = grad + jnp.concatenate([spread_mid(x[e * HD : (e + 1) * HD], 2 * p + e) for e in (0, 1)], axis=0)
        ostage[1, p] = grad.astype(BF).T
        out_start(1, p)
        for a, own in ((0, dk), (1, dv)):
            y = jnp.sum(trec[:, a, :, p * 128 : (p + 1) * 128].astype(F32), axis=0).astype(BF)
            y = jnp.concatenate([y] * 4, axis=0)
            grad = own[p] + dot(ett[...], keep(y, row_head == 2 * p + lane_odd))
            y = mout[d, a, p].astype(F32)
            for s in range(1, MIDDLE):
                y = y + mrec[s - 1, a, p].astype(F32)
            y = y.astype(BF)
            grads = []
            for j in range(NJ):
                z = y[j * 128 : (j + 1) * 128]
                z = jnp.concatenate([half_lanes(z, 0), half_lanes(z, 1)], axis=0)
                grads.append(grad[j * 512 : (j + 1) * 512] + dot(e2t[p], z))
            ostage[2 + a, p] = jnp.concatenate(grads, axis=0).astype(BF)
            out_start(2 + a, p)

    backward_one(0)

    def wait_part(s, carry):
        part_copy(s).wait_send()
        part_arrival(s).wait_recv()
        return carry

    lax.fori_loop(1, C, wait_part, 0)
    for s in range(1, MIDDLE):
        @pl.when(d >= s)
        def _():
            mid_part(s).wait_send()

        @pl.when(d + s < MIDDLE)
        def _():
            mid_part(s).wait_recv()

    finish(0)
    backward_one(1)
    finish(1)

    for a in range(4):
        for p in (0, 1):
            out_local(a, p).wait()
            for s in (1, 2, 3):
                out_copy(a, p, s).wait_send()
                out_arrival(a, p, s).wait_recv()


def solution(mesh):
    C, H = mesh.shape["ctx"], mesh.shape["head"]

    def shards(queries, keys, values, grad_out, offset_mid, head_top_offsets):
        T, W = queries.shape
        R = T * H
        MC, TC = R // MIDDLE, R // C
        TQ = 4 * TC
        shape = jax.ShapeDtypeStruct((T, W), BF)
        hbm = pl.BlockSpec(memory_space=pl.ANY)
        smem = pl.BlockSpec(memory_space=pltpu.SMEM)
        vm = pltpu.VMEM
        dma = pltpu.SemaphoreType.DMA
        scratch = [
            vm((4, 2, R, 128), BF),
            vm((4, 2, 128, R), BF),
            vm((4, R // 2, R + B), BF),
            vm((MIDDLE, 2, 2, MC, 128), BF),
            vm((MIDDLE, 2, 2, 128, MC), BF),
            vm((2, 2, 128, MC), BF),
            vm((4, MIDDLE, MC, MC), BF),
            vm((2, MIDDLE, MC, MC), F32),
            vm((C, 2, TC, 256), BF),
            vm((2, 256, R), BF),
            vm((2, TQ, 256), BF),
            vm((2, 256, TQ), BF),
            vm((R, TQ), BF),
            vm((2, 256, 512), BF),
            vm((2, 512, 256), BF),
            vm((TQ, R), BF),
            vm((R, TQ), BF),
            vm((256, R), F32),
            vm((256, MC), F32),
            vm((256, TQ), F32),
            vm((8, R), F32),
            vm((8, MC), F32),
            vm((8, TQ), F32),
            vm((8, R), F32),
            vm((8, MC), F32),
            vm((8, TQ), F32),
            vm((256, R), F32),
            vm((2, R, 128), F32),
            vm((2, R, 128), F32),
            vm((256, MC), F32),
            vm((256, TQ), F32),
            vm((MIDDLE, 2, 2, MC, 128), BF),
            vm((MIDDLE - 1, 2, 2, MC, 128), BF),
            vm((C, 2, TC, 256), BF),
            vm((C, 2, TC, 256), BF),
            vm((4, 2, R, 128), BF),
            dma((24,)), dma((24,)), dma((8,)),
            dma((3,)), dma((3,)), dma((3,)), dma((3,)),
            dma((C,)), dma((C,)), dma((C,)), dma((C,)),
            dma((24,)), dma((24,)), dma((8,)),
        ]
        return pl.pallas_call(
            functools.partial(kernel, C, H, T),
            out_shape=[shape] * 4,
            in_specs=[smem, smem, hbm, hbm, hbm, hbm],
            out_specs=[hbm] * 4,
            scratch_shapes=scratch,
            compiler_params=pltpu.CompilerParams(
                collective_id=0, has_side_effects=True, vmem_limit_bytes=62 << 20
            ),
        )(offset_mid, head_top_offsets, queries, keys, values, grad_out)

    rows = P(("ctx", "head"), None)
    return jax.shard_map(
        shards,
        mesh=mesh,
        in_specs=(rows, rows, rows, rows, P("head"), P("head")),
        out_specs=(rows,) * 4,
        check_vma=False,
    )
```

```python
import functools

import jax
import jax.numpy as jnp
from jax import lax
from jax.experimental import pallas as pl
from jax.experimental.pallas import tpu as pltpu
from jax.sharding import PartitionSpec as P

MESH = pl.DeviceIdType.MESH
HD = 64
MIDDLE = 4
B = 256
NEG = -1e30
F32 = jnp.float32
BF = jnp.bfloat16
Q, K, V, G = 0, 1, 2, 3


def dot(a, b):
    return jnp.dot(a, b, preferred_element_type=F32)


def iota(shape, dim):
    return lax.broadcasted_iota(jnp.int32, shape, dim)


def keep(x, mask):
    return jnp.where(mask, x, jnp.zeros_like(x))


def half_rows(x, e):
    return keep(x, (iota(x.shape, 0) >= HD) == (e == 1))


def half_lanes(x, e):
    return keep(x, (iota(x.shape, 1) >= HD) == (e == 1))


def swap_halves(x):
    return pltpu.roll(x.astype(F32), HD, 1)


def split3(x):
    hi = x.astype(BF).astype(F32)
    rest = x - hi
    mid = rest.astype(BF).astype(F32)
    return hi, mid, rest - mid


def stack_rows(rows, count):
    n = rows[0].shape[1]
    at = iota((count, n), 0)
    out = jnp.zeros((count, n), F32)
    for i, row in enumerate(rows):
        out = jnp.where(at == i, row, out)
    return out


def above(x):
    return jnp.concatenate([x, jnp.zeros_like(x)], axis=0)


def below(x):
    return jnp.concatenate([jnp.zeros_like(x), x], axis=0)


def kernel(
    C, T,
    off_in, q_in, k_in, v_in, g_in,
    o_out, dq_out, dk_out, dv_out,
    offs, xin, xt, pst, pc, pm, ptop, ehot, ehot_t,
    gsend, grecv, mqk, mvg, mqk_t, mvg_t, mq_w, mg_w, tqk, tvg, ttkv, ttkv_t,
    o1, ox, st1, stx, stm, stt, cd1, xo, sx_in, sx_out, om, oret, orecv, ssend, srecv,
    dqt, dk, dv, xdq, xdkv, dqm, gret, gback, tpart, trec, ostage,
    off_s, off_r, sw_s, sw_r, sw_l, xs, xr, gs, gr, ts, tr, os_, or_, xos, xor_,
    ss, sr, sxs, sxr, tps, tpr, rs, rr, xds, xdr, fs, fr, fl,
):
    N = 2 * T
    NB = N // B
    M = 8
    MR = N // MIDDLE
    TR = N // C
    CR = MR + 32
    R = M * MR
    MB = R // B
    TQ = M * 32
    c = lax.axis_index("ctx")
    h = lax.axis_index("head")
    core = lax.rem(h, 2)
    late = h // 2
    group = c // MIDDLE
    w = lax.rem(c, MIDDLE) * 2 + late
    groups = C // MIDDLE
    ins = (q_in, k_in, v_in, g_in)
    outs = (o_out, dq_out, dk_out, dv_out)
    mate = (c, h + 1 - 2 * core)
    far = (c, lax.rem(h + 2, 4))
    across = (c, 3 - h)

    def member(i):
        return (group * MIDDLE + i // 2, 2 * lax.rem(i, 2) + core)

    def at_group(g):
        return (g * MIDDLE + lax.rem(c, MIDDLE), h)

    bar = pltpu.get_barrier_semaphore()

    def greet(dev):
        pl.semaphore_signal(bar, inc=1, device_id=dev, device_id_type=MESH)

    greet(mate)
    greet(across)
    for s in range(1, M):
        greet(member(lax.rem(w + s, M)))
    for s in range(1, groups):
        greet(at_group(lax.rem(group + s, groups)))
    pl.semaphore_wait(bar, 2 + M - 1 + groups - 1)

    def remote(src, dst, ssem, rsem, dev):
        return pltpu.make_async_remote_copy(
            src_ref=src, dst_ref=dst, send_sem=ssem, recv_sem=rsem,
            device_id=dev, device_id_type=MESH,
        )

    def lanes(of, p):
        return pl.ds(pl.multiple_of(of * 512 + p * 128, 128), 128)

    mine = pl.ds(pl.multiple_of(core * T, T), T)
    theirs = pl.ds(pl.multiple_of((1 - core) * T, T), T)

    def off_copy(s):
        to = lax.rem(h + s, 4)
        return remote(off_in, offs.at[h], off_s.at[s - 1], off_r.at[s - 1], (c, to))

    def off_arrival(s):
        frm = lax.rem(h + 4 - s, 4)
        return remote(off_in, offs.at[frm], off_s.at[s - 1], off_r.at[s - 1], (c, lax.rem(h + s, 4)))

    for s in (1, 2, 3):
        off_copy(s).start()
    offs[h] = off_in[...]

    def swap_copy(a, p):
        i = a * 4 + p
        return remote(ins[a].at[:, lanes(1 - core, p)], xin.at[a, p, mine], sw_s.at[i], sw_r.at[i], mate)

    def swap_arrival(a, p):
        i = a * 4 + p
        return remote(ins[a].at[:, lanes(1 - core, p)], xin.at[a, p, theirs], sw_s.at[i], sw_r.at[i], mate)

    def swap_local(a, p):
        return pltpu.make_async_copy(ins[a].at[:, lanes(core, p)], xin.at[a, p, mine], sw_l.at[a * 4 + p])

    for a in (K, Q, V, G):
        for p in range(4):
            swap_copy(a, p).start()
            swap_local(a, p).start()

    def cross_copy(a, n, p, side):
        i = n * 4 + p * 2 + side
        pair = p if a in (K, V) else 2 + p
        of = core if side == 0 else 1 - core
        return remote(
            ins[a].at[:, lanes(of, pair)], xin.at[a, 4 + p, mine], xs.at[i], xr.at[i],
            far if side == 0 else across,
        )

    cross_kinds = ((0, (K, V)), (1, (Q, G)))
    for half, kinds in cross_kinds:
        @pl.when(late == half)
        def _():
            for p in (0, 1):
                for n, a in enumerate(kinds):
                    for side in (0, 1):
                        cross_copy(a, n, p, side).start()

    def cross_wait():
        for half, kinds in cross_kinds:
            @pl.when(late == half)
            def _():
                for p in (0, 1):
                    for n, a in enumerate(kinds):
                        for side in (0, 1):
                            cross_copy(a, n, p, side).wait_send()
                for p in (0, 1):
                    for n, a in enumerate(cross_kinds[1 - half][1]):
                        for side in (0, 1):
                            i = n * 4 + p * 2 + side
                            remote(
                                ins[a].at[:, lanes(core, p)],
                                xin.at[a, 4 + p, mine if side == 0 else theirs],
                                xs.at[i], xr.at[i], far if side == 0 else across,
                            ).wait_recv()

    for s in (1, 2, 3):
        off_copy(s).wait_send()
        off_arrival(s).wait_recv()
    r = iota((CR, N), 0)
    first = r < MR
    row_from = iota((CR, N), 1) - jnp.where(
        first, MIDDLE * r, jnp.where(r < MR + TR, C * (r - MR), -1000000)
    )
    r = iota((1, CR), 1)
    lane_first = r < MR
    lane_to = jnp.where(lane_first, MIDDLE * r, jnp.where(r < MR + TR, C * (r - MR), -1000000))
    token_row = iota((N, CR), 0)
    token = iota((1, N), 1)
    off_mid, off_top = [], []
    for hd in range(8):
        of = 2 * core + hd // 4
        j = hd % 4
        mid_row = offs[of, j : j + 1, :]
        top_row = offs[of, 4 + j : 5 + j, :]
        mid_n = jnp.concatenate([mid_row] * (N // 128), axis=1)
        top_n = jnp.concatenate([top_row] * (N // 128), axis=1)
        off_mid.append(mid_n)
        off_top.append(top_n)
        ehot[hd] = (row_from == jnp.where(first, mid_n, top_n)).astype(F32).astype(BF)
        goal = lane_to + jnp.where(lane_first, mid_n[:, :CR], top_n[:, :CR])
        ehot_t[hd] = (token_row == goal).astype(F32).astype(BF)

    for a in (K, Q, V, G):
        for p in range(4):
            swap_local(a, p).wait()
            swap_copy(a, p).wait_send()
            swap_arrival(a, p).wait_recv()

    low = iota((CR, 128), 1) < HD
    for p in range(4):
        for n, (a, b) in enumerate(((Q, K), (V, G))):
            x = jnp.concatenate([xin[a, p], xin[b, p]], axis=1)
            for e in (0, 1):
                t = dot(ehot[2 * p + e], x)
                if e == 0:
                    t = jnp.where(low, t[:, :128], swap_halves(t[:, 128:]))
                else:
                    t = jnp.where(low, swap_halves(t[:, :128]), t[:, 128:])
                gsend[2 * p + e, :, n * 128 : (n + 1) * 128] = t.astype(BF)

    def to_members(src, dst, ssem, rsem):
        def copy(s):
            to = lax.rem(w + s, M)
            return remote(src.at[to], dst.at[w], ssem.at[s - 1], rsem.at[s - 1], member(to))

        def arrival(s):
            frm = lax.rem(w + M - s, M)
            return remote(src.at[frm], dst.at[frm], ssem.at[s - 1], rsem.at[s - 1], member(lax.rem(w + s, M)))

        def start():
            for s in range(1, M):
                copy(s).start()
            dst[w] = src[w]

        def wait():
            for s in range(1, M):
                copy(s).wait_send()
                arrival(s).wait_recv()

        return start, wait

    g_start, g_wait = to_members(gsend, grecv, gs, gr)
    o_start, o_wait = to_members(oret, orecv, os_, or_)
    s_start, s_wait = to_members(ssend, srecv, ss, sr)
    r_start, r_wait = to_members(gret, gback, rs, rr)
    g_start()

    for a in (K, Q, V, G):
        for p in range(4):
            x = xin[a, p]
            xt[a, p] = (x * 0.125).T if a == Q else x.T

    causal = iota((B, B), 0) <= iota((B, B), 1)

    def softmax_block(s, i):
        n = s.shape[0]
        chunks = [s[b * B : (b + 1) * B] for b in range(n // B)]
        if i is not None:
            chunks[-1] = jnp.where(causal, chunks[-1], NEG)
        m = jnp.max(chunks[0], axis=0, keepdims=True)
        for x in chunks[1:]:
            m = jnp.maximum(m, jnp.max(x, axis=0, keepdims=True))
        total = None
        parts = []
        for x in chunks:
            x = jnp.exp(x - m)
            t = jnp.sum(x, axis=0, keepdims=True)
            total = t if total is None else total + t
            parts.append(x.astype(BF))
        return m, total, parts

    def join(parts):
        return parts[0] if len(parts) == 1 else jnp.concatenate(parts, axis=0)

    def place_one(kb, i):
        if kb == 0:
            return 0, i * B
        return B, (i - 1) * B if kb == 1 else 2 * B

    def one_block(hh, kb, i):
        r, l = place_one(kb, i)
        return pst.at[hh, r : r + B, l : l + B]

    def one_tail(hh, kb):
        r, l = place_one(kb, kb)
        return pst[hh, r : r + B, l : l + (NB - kb) * B]

    def forward_one(p):
        for i in range(NB):
            n = (i + 1) * B
            for e in (0, 1):
                hh = 2 * p + e
                s = dot(xin[K, p, :n], half_rows(xt[Q, p, :, i * B : n], e))
                m, total, parts = softmax_block(s, i)
                for kb in range(i + 1):
                    one_block(hh, kb, i)[...] = parts[kb]
                o1[hh * HD : (hh + 1) * HD, i * B : n] = dot(xt[V, p, e * HD : (e + 1) * HD, :n], join(parts))
                st1[hh : hh + 1, i * B : n] = m
                st1[8 + hh : 9 + hh, i * B : n] = total

    for p in range(4):
        forward_one(p)

    g_wait()
    for i in range(M):
        mqk[i * MR : (i + 1) * MR] = grecv[i, :MR, :128]
        mvg[i * MR : (i + 1) * MR] = grecv[i, :MR, 128:]
        tqk[i * 32 : (i + 1) * 32] = grecv[i, MR:, :128]
        tvg[i * 32 : (i + 1) * 32] = grecv[i, MR:, 128:]
    ttkv[group] = jnp.where(iota((TQ, 128), 1) < HD, tvg[...], tqk[...])

    def top_copy(s):
        return remote(ttkv.at[group], ttkv.at[group], ts.at[s - 1], tr.at[s - 1], at_group(lax.rem(group + s, groups)))

    def top_arrival(s):
        frm = lax.rem(group + groups - s, groups)
        return remote(ttkv.at[frm], ttkv.at[frm], ts.at[s - 1], tr.at[s - 1], at_group(lax.rem(group + s, groups)))

    for s in range(1, groups):
        @pl.when(group + s < groups)
        def _():
            top_copy(s).start()

    def clear(g, carry):
        ttkv[g] = jnp.zeros((TQ, 128), BF)
        return carry

    lax.fori_loop(group + 1, groups, clear, 0)

    cross_wait()
    first_kind = late
    second_kind = 3 - late
    scale = jnp.where(late == 0, 0.125, 1.0).astype(F32)
    kv_slot = jnp.where(late == 0, 2, 4)
    qg_slot = jnp.where(late == 0, 4, 0)
    for p in (0, 1):
        xt[first_kind, 4 + p] = (xin[first_kind, 4 + p].astype(F32) * scale).astype(BF).T
        xt[second_kind, 4 + p] = xin[second_kind, 4 + p].T
    for p in (0, 1):
        kv, qg = kv_slot + p, qg_slot + p
        for i in range(NB):
            at = slice(i * B, (i + 1) * B)
            for e in (0, 1):
                hh = 2 * p + e
                m, total, parts = softmax_block(dot(xin[K, kv], half_rows(xt[Q, qg, :, at], e)), None)
                wts = join(parts)
                pc[hh, :, at] = wts
                ox[hh * HD : (hh + 1) * HD, at] = dot(xt[V, kv, e * HD : (e + 1) * HD, :], wts)
                stx[hh : hh + 1, at] = m
                stx[4 + hh : 5 + hh, at] = total
    logs = []
    for hh in range(4):
        rows = slice(hh * HD, (hh + 1) * HD)
        total = stx[4 + hh : 5 + hh]
        xo[0, rows] = (ox[rows] / total).astype(BF)
        logs += list(split3(stx[hh : hh + 1] + jnp.log(total)))
    xo[0, 256:272] = stack_rows(logs, 16).astype(BF)

    xo_copy = remote(xo.at[0], xo.at[1], xos.at[0], xor_.at[0], far)

    @pl.when(late == 0)
    def _():
        xo_copy.start()
        xo[1] = jnp.zeros(xo.shape[1:], BF)

    def place_mid(kb, i):
        if kb < MB // 2:
            return kb * B, (i - kb) * B
        return (MB - 1 - kb) * B, (i + 1) * B

    def mid_block(kb, i):
        r, l = place_mid(kb, i)
        return pm.at[r : r + B, l : l + B]

    def mid_tail(kb):
        r, l = place_mid(kb, kb)
        return pm[r : r + B, l : l + (MB - kb) * B]

    mqk_t[...] = mqk[...].T
    mvg_t[...] = mvg[...].T
    mq_w[...] = below(mqk_t[:HD] * 0.125)
    mg_w[...] = above(mvg_t[HD:])
    for i in range(MB):
        n = (i + 1) * B
        at = slice(i * B, n)
        m, total, parts = softmax_block(dot(mqk[:n], mq_w[:, at]), i)
        for kb in range(i + 1):
            mid_block(kb, i)[...] = parts[kb]
        om[:HD, at] = dot(mvg_t[:HD, :n], join(parts)) / total
        om[HD:, at] = stack_rows(split3(m + jnp.log(total)), HD)
        stm[0:1, at] = m
        stm[1:2, at] = total
    x = om[...].astype(BF).T
    for i in range(M):
        oret[i, :MR] = x[i * MR : (i + 1) * MR]

    for s in range(1, groups):
        @pl.when(group + s < groups)
        def _():
            top_copy(s).wait_send()

        @pl.when(group >= s)
        def _():
            top_arrival(s).wait_recv()

    keys_n = groups * TQ
    kv_top = ttkv[...].reshape(keys_n, 128)
    ttkv_t[...] = kv_top.T
    tqk_t = tqk[...].T
    tq_w = below(tqk_t[:HD] * 0.125)
    tg_w = above(tvg[...].T[HD:])
    r = iota((keys_n, 1), 0)
    key_rank = jnp.where(
        (r & 31) < TR, (r >> 8) * (M * TR) + ((r >> 5) & 7) * TR + (r & 31), 1000000
    )
    r = iota((1, TQ), 1)
    query_rank = group * (M * TR) + (r >> 5) * TR + (r & 31)
    s = jnp.where(key_rank <= query_rank, dot(kv_top, tq_w), NEG)
    m, total, parts = softmax_block(s, None)
    x = join(parts)
    ptop[...] = x
    out = dot(ttkv_t[:HD], x) / total
    x = jnp.concatenate([out, stack_rows(split3(m + jnp.log(total)), HD)], axis=0).astype(BF).T
    for i in range(M):
        oret[i, MR:] = x[i * 32 : (i + 1) * 32]
    stt[0:1] = total
    o_start()

    @pl.when(late == 0)
    def _():
        xo_copy.wait_send()

    @pl.when(late == 1)
    def _():
        xo_copy.wait_recv()

    o_wait()
    lane_mid = iota((80, CR), 1) < MR

    def out_copy(a, p):
        i = a * 4 + p
        return remote(ostage.at[a, p, theirs], outs[a].at[:, lanes(core, p)], fs.at[i], fr.at[i], mate)

    def out_arrival(a, p):
        i = a * 4 + p
        return remote(ostage.at[a, p, theirs], outs[a].at[:, lanes(1 - core, p)], fs.at[i], fr.at[i], mate)

    def out_local(a, p):
        return pltpu.make_async_copy(ostage.at[a, p, mine], outs[a].at[:, lanes(core, p)], fl.at[a * 4 + p])

    def out_start(a, p):
        out_copy(a, p).start()
        out_local(a, p).start()

    for hh in range(8):
        p, e = hh // 2, hh % 2
        rows = slice(hh * HD, (hh + 1) * HD)
        x = orecv[hh].T[:80]
        x = jnp.concatenate([keep(x, lane_mid), keep(x, ~lane_mid)], axis=0)
        x = dot(x, ehot[hh])
        out_m, out_t = x[:HD], x[80 : 80 + HD]
        log_m = x[64:65] + x[65:66] + x[66:67]
        log_t = x[144:145] + x[145:146] + x[146:147]
        log_m = jnp.where((token & (MIDDLE - 1)) == off_mid[hh], log_m, NEG)
        log_t = jnp.where((token & (C - 1)) == off_top[hh], log_t, NEG)
        j = hh % 4
        out_x = xo[hh // 4, j * HD : (j + 1) * HD].astype(F32)
        x = xo[hh // 4, 256:272].astype(F32)
        log_x = x[3 * j : 3 * j + 1] + x[3 * j + 1 : 3 * j + 2] + x[3 * j + 2 : 3 * j + 3]
        log_x = jnp.where(late == 1, log_x, NEG)
        total = st1[8 + hh : 9 + hh]
        log_1 = st1[hh : hh + 1] + jnp.log(total)
        peak = jnp.maximum(jnp.maximum(log_1, log_x), jnp.maximum(log_m, log_t))
        e_1, e_x = jnp.exp(log_1 - peak), jnp.exp(log_x - peak)
        e_m, e_t = jnp.exp(log_m - peak), jnp.exp(log_t - peak)
        norm = e_1 + e_x + e_m + e_t
        s_x, s_m, s_t = e_x / norm, e_m / norm, e_t / norm
        c_1 = e_1 / norm / total
        mixed = c_1 * o1[rows] + s_x * out_x + s_m * out_m + s_t * out_t
        o1[rows] = mixed
        delta = jnp.sum(xt[G, p, e * HD : (e + 1) * HD].astype(F32) * mixed, axis=0, keepdims=True)
        cd1[hh : hh + 1] = c_1
        cd1[8 + hh : 9 + hh] = delta
        stats = stack_rows(split3(s_m) + split3(s_t) + split3(delta), 16).astype(BF)
        g = dot(stats, ehot_t[hh])
        share = jnp.where(lane_first, g[0:1] + g[1:2] + g[2:3], g[3:4] + g[4:5] + g[5:6])
        ssend[hh, :, :CR] = stack_rows((share, g[6:7] + g[7:8] + g[8:9]), 8)
        if hh < 4:
            @pl.when(late == 1)
            def _():
                sx_in[j : j + 1] = s_x
                sx_in[4 + j : 5 + j] = delta
        else:
            sx_out[j : j + 1] = s_x
            sx_out[4 + j : 5 + j] = delta
        if e == 1:
            ostage[0, p] = o1[p * 128 : (p + 1) * 128].astype(BF).T
            out_start(0, p)

    sx_copy = remote(sx_out, sx_in, sxs.at[0], sxr.at[0], far)

    @pl.when(late == 1)
    def _():
        sx_copy.start()

    s_start()

    def scaled(x, c_low, c_high):
        return (x.astype(F32) * jnp.where(iota(x.shape, 0) < HD, c_low, c_high)).astype(BF).T

    def backward_one(p):
        cs = (cd1[2 * p : 2 * p + 1], cd1[2 * p + 1 : 2 * p + 2])
        gc, qc = scaled(xt[G, p], *cs), scaled(xt[Q, p], *cs)
        gcs = [half_lanes(gc, e) for e in (0, 1)]
        qcs = [half_lanes(qc, e) for e in (0, 1)]
        for kb in range(NB):
            dv[p, kb * B : (kb + 1) * B] = dot(one_tail(2 * p, kb), gcs[0][kb * B :]) + dot(
                one_tail(2 * p + 1, kb), gcs[1][kb * B :]
            )
        for i in range(NB):
            n = (i + 1) * B
            for e in (0, 1):
                hh = 2 * p + e
                dp = dot(xin[V, p, :n], half_rows(xt[G, p, :, i * B : n], e))
                delta = cd1[8 + hh : 9 + hh, i * B : n]
                parts = []
                for kb in range(i + 1):
                    x = one_block(hh, kb, i)[...].astype(F32)
                    x = (x * (dp[kb * B : (kb + 1) * B] - delta)).astype(BF)
                    one_block(hh, kb, i)[...] = x
                    parts.append(x)
                dqt[hh * HD : (hh + 1) * HD, i * B : n] = dot(
                    xt[K, p, e * HD : (e + 1) * HD, :n], join(parts)
                ) * (cs[e][:, i * B : n] * 0.125)
        for kb in range(NB):
            dk[p, kb * B : (kb + 1) * B] = dot(one_tail(2 * p, kb), qcs[0][kb * B :]) + dot(
                one_tail(2 * p + 1, kb), qcs[1][kb * B :]
            )

    backward_one(0)

    @pl.when(late == 1)
    def _():
        sx_copy.wait_send()

    @pl.when(late == 0)
    def _():
        sx_copy.wait_recv()

    xdq_copy = remote(xdq.at[0], xdq.at[1], xds.at[4], xdr.at[4], far)

    def xdkv_copy(n, p):
        i = n * 2 + p
        return remote(xdkv.at[0, n, p], xdkv.at[1, n, p], xds.at[i], xdr.at[i], far)

    for p in (0, 1):
        kv, qg = kv_slot + p, qg_slot + p
        cs = [sx_in[2 * p + e : 2 * p + e + 1] / stx[4 + 2 * p + e : 5 + 2 * p + e] for e in (0, 1)]
        gc, qc = scaled(xt[G, qg], *cs), scaled(xt[Q, qg], *cs)
        xdkv[0, 1, p] = (dot(pc[2 * p], half_lanes(gc, 0)) + dot(pc[2 * p + 1], half_lanes(gc, 1))).astype(BF)

        @pl.when(late == 1)
        def _():
            xdkv_copy(1, p).start()

        for i in range(NB):
            at = slice(i * B, (i + 1) * B)
            for e in (0, 1):
                hh = 2 * p + e
                dp = dot(xin[V, kv], half_rows(xt[G, qg, :, at], e))
                x = (pc[hh, :, at].astype(F32) * (dp - sx_in[4 + hh : 5 + hh, at])).astype(BF)
                pc[hh, :, at] = x
                x = dot(xt[K, kv, e * HD : (e + 1) * HD, :], x) * (cs[e][:, at] * 0.125)
                xdq[0, hh * HD : (hh + 1) * HD, at] = x.astype(BF)
        xdkv[0, 0, p] = (dot(pc[2 * p], half_lanes(qc, 0)) + dot(pc[2 * p + 1], half_lanes(qc, 1))).astype(BF)

        @pl.when(late == 1)
        def _():
            xdkv_copy(0, p).start()

    @pl.when(late == 0)
    def _():
        xdq_copy.start()

    s_wait()
    t_stats = jnp.concatenate([srecv[i, :, MR:CR] for i in range(M)], axis=1)
    m_stats = jnp.concatenate([srecv[i, :, :MR] for i in range(M)], axis=1)
    t_c = t_stats[0:1] / stt[0:1]
    kv_top = ttkv[...].reshape(keys_n, 128)
    dp = dot(kv_top, tg_w)
    ds = (ptop[...].astype(F32) * (dp - t_stats[1:2])).astype(BF)
    t_dq = above(dot(ttkv_t[HD:], ds) * (t_c * 0.125)).astype(BF).T
    gc = above((tg_w[:HD].astype(F32) * t_c).astype(BF)).T
    qc = below((tq_w[HD:].astype(F32) * t_c).astype(BF)).T
    tpart[...] = (dot(ptop[...], gc) + dot(ds, qc)).astype(BF).reshape(groups, TQ, 128)

    def part_copy(s):
        to = lax.rem(group + groups - s, groups)
        return remote(tpart.at[to], trec.at[group], tps.at[s - 1], tpr.at[s - 1], at_group(to))

    def part_arrival(s):
        frm = lax.rem(group + s, groups)
        return remote(tpart.at[frm], trec.at[frm], tps.at[s - 1], tpr.at[s - 1], at_group(lax.rem(group + groups - s, groups)))

    for s in range(1, groups):
        @pl.when(group >= s)
        def _():
            part_copy(s).start()

    m_c = m_stats[0:1] / stm[1:2]
    gc = above((mg_w[:HD].astype(F32) * m_c).astype(BF)).T
    qc = below((mq_w[HD:].astype(F32) * m_c).astype(BF)).T
    m_dv = [dot(mid_tail(kb), gc[kb * B :]) for kb in range(MB)]
    for i in range(MB):
        n = (i + 1) * B
        at = slice(i * B, n)
        dp = dot(mvg[:n], mg_w[:, at])
        parts = []
        for kb in range(i + 1):
            x = mid_block(kb, i)[...].astype(F32)
            x = (x * (dp[kb * B : (kb + 1) * B] - m_stats[1:2, at])).astype(BF)
            mid_block(kb, i)[...] = x
            parts.append(x)
        dqm[:, at] = dot(mqk_t[HD:, :n], join(parts)) * (m_c[:, at] * 0.125)
    m_vk = [m_dv[kb] + dot(mid_tail(kb), qc[kb * B :]) for kb in range(MB)]
    m_vk = jnp.concatenate(m_vk, axis=0).astype(BF)
    m_dq = above(dqm[...]).astype(BF).T
    for i in range(M):
        gret[i, :MR, :128] = m_vk[i * MR : (i + 1) * MR]
        gret[i, :MR, 128:] = m_dq[i * MR : (i + 1) * MR]
        gret[i, MR:, 128:] = t_dq[i * 32 : (i + 1) * 32]
    for s in range(1, groups):
        @pl.when(group >= s)
        def _():
            part_copy(s).wait_send()

        @pl.when(group + s < groups)
        def _():
            part_arrival(s).wait_recv()

    def add_part(g, x):
        return x + trec[g].astype(F32)

    x = lax.fori_loop(group + 1, groups, add_part, tpart[group].astype(F32)).astype(BF)
    for i in range(M):
        gret[i, MR:, :128] = x[i * 32 : (i + 1) * 32]
    r_start()

    backward_one(1)
    backward_one(2)
    backward_one(3)

    @pl.when(late == 0)
    def _():
        xdq_copy.wait_send()
        for n in (0, 1):
            for p in (0, 1):
                xdkv_copy(n, p).wait_recv()

    @pl.when(late == 1)
    def _():
        xdq_copy.wait_recv()
        for n in (0, 1):
            for p in (0, 1):
                xdkv_copy(n, p).wait_send()

    r_wait()
    for p in range(4):
        rows = slice(p * 128, (p + 1) * 128)

        @pl.when(late == 1)
        def _():
            dqt[rows] += xdq[p // 2, (p % 2) * 128 : (p % 2 + 1) * 128].astype(F32)

        @pl.when(late == 0)
        def _():
            dk[p] += xdkv[1 - p // 2, 0, p % 2].astype(F32)
            dv[p] += xdkv[1 - p // 2, 1, p % 2].astype(F32)

        sums = None
        for e in (0, 1):
            y = gback[2 * p + e]
            vk, yq = y[:, :128], y[:, 128:]
            turned = swap_halves(vk).astype(BF)
            if e == 0:
                y = (half_lanes(vk, 0), half_lanes(turned, 0), yq)
            else:
                y = (half_lanes(turned, 1), half_lanes(vk, 1), swap_halves(yq).astype(BF))
            t = dot(ehot_t[2 * p + e], jnp.concatenate(y, axis=1))
            sums = t if sums is None else sums + t
        ostage[1, p] = (dqt[rows].T + sums[:, 256:]).astype(BF)
        ostage[2, p] = (dk[p] + sums[:, 128:256]).astype(BF)
        ostage[3, p] = (dv[p] + sums[:, :128]).astype(BF)
        for a in (1, 2, 3):
            out_start(a, p)

    for a in range(4):
        for p in range(4):
            out_local(a, p).wait()
            out_copy(a, p).wait_send()
            out_arrival(a, p).wait_recv()


def solution(mesh):
    C = mesh.shape["ctx"]

    def shards(queries, keys, values, grad_out, offset_mid, head_top_offsets):
        T, W = queries.shape
        N = 2 * T
        CR = N // MIDDLE + 32
        R = 8 * (N // MIDDLE)
        TK = C // MIDDLE * 256
        shape = jax.ShapeDtypeStruct((T, W), BF)
        hbm = pl.BlockSpec(memory_space=pl.ANY)
        vm = pltpu.VMEM
        dma = pltpu.SemaphoreType.DMA
        offsets = jnp.concatenate([offset_mid, head_top_offsets])
        offsets = jnp.broadcast_to(offsets[:, None], (8, 128))
        scratch = [
            vm((4, 8, 128), jnp.int32),
            vm((4, 6, N, 128), BF),
            vm((4, 6, 128, N), BF),
            vm((8, 2 * B, N), BF),
            vm((4, N, N), BF),
            vm((R // 2, R + B), BF),
            vm((TK, 256), BF),
            vm((8, CR, N), BF),
            vm((8, N, CR), BF),
            vm((8, CR, 256), BF),
            vm((8, CR, 256), BF),
            vm((R, 128), BF),
            vm((R, 128), BF),
            vm((128, R), BF),
            vm((128, R), BF),
            vm((128, R), BF),
            vm((128, R), BF),
            vm((256, 128), BF),
            vm((256, 128), BF),
            vm((C // MIDDLE, 256, 128), BF),
            vm((128, TK), BF),
            vm((512, N), F32),
            vm((256, N), F32),
            vm((16, N), F32),
            vm((8, N), F32),
            vm((8, R), F32),
            vm((8, 256), F32),
            vm((16, N), F32),
            vm((2, 272, N), BF),
            vm((8, N), F32),
            vm((8, N), F32),
            vm((128, R), F32),
            vm((8, CR, 128), BF),
            vm((8, CR, 128), BF),
            vm((8, 8, 256), F32),
            vm((8, 8, 256), F32),
            vm((512, N), F32),
            vm((4, N, 128), F32),
            vm((4, N, 128), F32),
            vm((2, 256, N), BF),
            vm((2, 2, 2, N, 128), BF),
            vm((HD, R), F32),
            vm((8, CR, 256), BF),
            vm((8, CR, 256), BF),
            vm((C // MIDDLE, 256, 128), BF),
            vm((C // MIDDLE, 256, 128), BF),
            vm((4, 4, N, 128), BF),
            dma((3,)), dma((3,)), dma((16,)), dma((16,)), dma((16,)),
            dma((8,)), dma((8,)), dma((7,)), dma((7,)), dma((7,)), dma((7,)),
            dma((7,)), dma((7,)), dma((1,)), dma((1,)), dma((7,)), dma((7,)),
            dma((1,)), dma((1,)), dma((7,)), dma((7,)), dma((7,)), dma((7,)),
            dma((5,)), dma((5,)), dma((16,)), dma((16,)), dma((16,)),
        ]
        return pl.pallas_call(
            functools.partial(kernel, C, T),
            out_shape=[shape] * 4,
            in_specs=[pl.BlockSpec(memory_space=pltpu.VMEM), hbm, hbm, hbm, hbm],
            out_specs=[hbm] * 4,
            scratch_shapes=scratch,
            compiler_params=pltpu.CompilerParams(
                collective_id=0, has_side_effects=True, vmem_limit_bytes=62 << 20
            ),
        )(offsets, queries, keys, values, grad_out)

    rows = P(("ctx", "head"), None)
    return jax.shard_map(
        shards,
        mesh=mesh,
        in_specs=(rows, rows, rows, rows, P("head"), P("head")),
        out_specs=(rows,) * 4,
        check_vma=False,
    )
```

```python
import functools

import jax
import jax.numpy as jnp
from jax import lax
from jax.experimental import pallas as pl
from jax.experimental.pallas import tpu as pltpu
from jax.sharding import PartitionSpec as P

MESH = pl.DeviceIdType.MESH
HD = 64
MIDDLE = 4
B = 256
NEG = -1e30
F32 = jnp.float32
BF = jnp.bfloat16
Q, K, V, G = 0, 1, 2, 3


def dot(a, b):
    return jnp.dot(a, b, preferred_element_type=F32)


def iota(shape, dim):
    return lax.broadcasted_iota(jnp.int32, shape, dim)


def keep(x, mask):
    return jnp.where(mask, x, jnp.zeros_like(x))


def half_rows(x, e):
    return keep(x, (iota(x.shape, 0) >= HD) == (e == 1))


def half_lanes(x, e):
    return keep(x, (iota(x.shape, 1) >= HD) == (e == 1))


def swap_halves(x):
    return pltpu.roll(x.astype(F32), HD, 1)


def split3(x):
    hi = x.astype(BF).astype(F32)
    rest = x - hi
    mid = rest.astype(BF).astype(F32)
    return hi, mid, rest - mid


def stack_rows(rows, count):
    n = rows[0].shape[1]
    at = iota((count, n), 0)
    out = jnp.zeros((count, n), F32)
    for i, row in enumerate(rows):
        out = jnp.where(at == i, row, out)
    return out


def above(x):
    return jnp.concatenate([x, jnp.zeros_like(x)], axis=0)


def below(x):
    return jnp.concatenate([jnp.zeros_like(x), x], axis=0)


def kernel(
    C, T,
    mid_in, top_in, q_in, k_in, v_in, g_in,
    o_out, dq_out, dk_out, dv_out,
    off_in, offs, xin, xt, pst, pc, pm, ptop, ehot, ehot_t,
    gsend, grecv, mqk, mvg, mqk_t, mvg_t, mq_w, mg_w, tqk, tvg, ttkv, ttkv_t,
    o1, ox, st1, stx, stm, stt, cd1, xo, sx_in, sx_out, om, oret, orecv, ssend, srecv,
    dqt, dk, dv, xdq, xdkv, dqm, gret, gback, tpart, trec, ostage,
    off_s, off_r, sw_s, sw_r, sw_l, xs, xr, gs, gr, ts, tr, os_, or_, xos, xor_,
    ss, sr, sxs, sxr, tps, tpr, rs, rr, xds, xdr, fs, fr, fl,
):
    N = 2 * T
    NB = N // B
    M = 8
    MR = N // MIDDLE
    TR = N // C
    CR = MR + 32
    R = M * MR
    MB = R // B
    TQ = M * 32
    c = lax.axis_index("ctx")
    h = lax.axis_index("head")
    core = lax.rem(h, 2)
    late = h // 2
    group = c // MIDDLE
    w = lax.rem(c, MIDDLE) * 2 + late
    groups = C // MIDDLE
    ins = (q_in, k_in, v_in, g_in)
    outs = (o_out, dq_out, dk_out, dv_out)
    mate = (c, h + 1 - 2 * core)
    far = (c, lax.rem(h + 2, 4))
    across = (c, 3 - h)

    def member(i):
        return (group * MIDDLE + i // 2, 2 * lax.rem(i, 2) + core)

    def at_group(g):
        return (g * MIDDLE + lax.rem(c, MIDDLE), h)

    bar = pltpu.get_barrier_semaphore()

    def greet(dev):
        pl.semaphore_signal(bar, inc=1, device_id=dev, device_id_type=MESH)

    greet(mate)
    greet(across)
    for s in range(1, M):
        greet(member(lax.rem(w + s, M)))
    for s in range(1, groups):
        greet(at_group(lax.rem(group + s, groups)))
    pl.semaphore_wait(bar, 2 + M - 1 + groups - 1)

    def remote(src, dst, ssem, rsem, dev):
        return pltpu.make_async_remote_copy(
            src_ref=src, dst_ref=dst, send_sem=ssem, recv_sem=rsem,
            device_id=dev, device_id_type=MESH,
        )

    def lanes(of, p):
        return pl.ds(pl.multiple_of(of * 512 + p * 128, 128), 128)

    mine = pl.ds(pl.multiple_of(core * T, T), T)
    theirs = pl.ds(pl.multiple_of((1 - core) * T, T), T)

    def off_copy(s):
        to = lax.rem(h + s, 4)
        return remote(off_in, offs.at[h], off_s.at[s - 1], off_r.at[s - 1], (c, to))

    def off_arrival(s):
        frm = lax.rem(h + 4 - s, 4)
        return remote(off_in, offs.at[frm], off_s.at[s - 1], off_r.at[s - 1], (c, lax.rem(h + s, 4)))

    for j in range(4):
        off_in[j : j + 1] = jnp.full((1, 128), mid_in[j], jnp.int32)
        off_in[4 + j : 5 + j] = jnp.full((1, 128), top_in[j], jnp.int32)
    for s in (1, 2, 3):
        off_copy(s).start()
    offs[h] = off_in[...]

    def swap_copy(a, p):
        i = a * 4 + p
        return remote(ins[a].at[:, lanes(1 - core, p)], xin.at[a, p, mine], sw_s.at[i], sw_r.at[i], mate)

    def swap_arrival(a, p):
        i = a * 4 + p
        return remote(ins[a].at[:, lanes(1 - core, p)], xin.at[a, p, theirs], sw_s.at[i], sw_r.at[i], mate)

    def swap_local(a, p):
        return pltpu.make_async_copy(ins[a].at[:, lanes(core, p)], xin.at[a, p, mine], sw_l.at[a * 4 + p])

    for a in (K, Q, V, G):
        for p in range(4):
            swap_copy(a, p).start()
            swap_local(a, p).start()

    waves = (
        (((K, 0), (V, 0)), ((Q, 0), (Q, 1))),
        (((K, 1), (V, 1)), ((G, 0), (G, 1))),
    )

    def cross_copy(wave, n, a, p, side):
        i = wave * 4 + n * 2 + side
        pair = p if a in (K, V) else 2 + p
        of = core if side == 0 else 1 - core
        return remote(
            ins[a].at[:, lanes(of, pair)], xin.at[a, 4 + p, mine], xs.at[i], xr.at[i],
            far if side == 0 else across,
        )

    def cross_arrival(wave, n, a, p, side):
        i = wave * 4 + n * 2 + side
        return remote(
            ins[a].at[:, lanes(core, p)], xin.at[a, 4 + p, mine if side == 0 else theirs],
            xs.at[i], xr.at[i], far if side == 0 else across,
        )

    def cross_start(wave):
        for half in (0, 1):
            @pl.when(late == half)
            def _():
                for n, (a, p) in enumerate(waves[wave][half]):
                    for side in (0, 1):
                        cross_copy(wave, n, a, p, side).start()

    def cross_wait(wave):
        for half in (0, 1):
            @pl.when(late == half)
            def _():
                for side in (0, 1):
                    for n, (a, p) in enumerate(waves[wave][half]):
                        cross_copy(wave, n, a, p, side).wait_send()
                    for n, (a, p) in enumerate(waves[wave][1 - half]):
                        cross_arrival(wave, n, a, p, side).wait_recv()

    cross_start(0)

    for s in (1, 2, 3):
        off_copy(s).wait_send()
        off_arrival(s).wait_recv()
    r = iota((CR, N), 0)
    first = r < MR
    row_from = iota((CR, N), 1) - jnp.where(
        first, MIDDLE * r, jnp.where(r < MR + TR, C * (r - MR), -1000000)
    )
    r = iota((1, CR), 1)
    lane_first = r < MR
    lane_to = jnp.where(lane_first, MIDDLE * r, jnp.where(r < MR + TR, C * (r - MR), -1000000))
    token_row = iota((N, CR), 0)
    token = iota((1, N), 1)
    off_mid, off_top = [], []
    for hd in range(8):
        of = 2 * core + hd // 4
        j = hd % 4
        mid_row = offs[of, j : j + 1, :]
        top_row = offs[of, 4 + j : 5 + j, :]
        mid_n = jnp.concatenate([mid_row] * (N // 128), axis=1)
        top_n = jnp.concatenate([top_row] * (N // 128), axis=1)
        off_mid.append(mid_n)
        off_top.append(top_n)
        ehot[hd] = (row_from == jnp.where(first, mid_n, top_n)).astype(F32).astype(BF)
        goal = lane_to + jnp.where(lane_first, mid_n[:, :CR], top_n[:, :CR])
        ehot_t[hd] = (token_row == goal).astype(F32).astype(BF)

    for a in (K, Q, V, G):
        for p in range(4):
            swap_local(a, p).wait()
            swap_copy(a, p).wait_send()
            swap_arrival(a, p).wait_recv()

    low = iota((CR, 128), 1) < HD
    for p in range(4):
        for n, (a, b) in enumerate(((Q, K), (V, G))):
            x = jnp.concatenate([xin[a, p], xin[b, p]], axis=1)
            for e in (0, 1):
                t = dot(ehot[2 * p + e], x)
                if e == 0:
                    t = jnp.where(low, t[:, :128], swap_halves(t[:, 128:]))
                else:
                    t = jnp.where(low, swap_halves(t[:, :128]), t[:, 128:])
                gsend[2 * p + e, :, n * 128 : (n + 1) * 128] = t.astype(BF)

    def to_members(src, dst, ssem, rsem):
        def copy(s):
            to = lax.rem(w + s, M)
            return remote(src.at[to], dst.at[w], ssem.at[s - 1], rsem.at[s - 1], member(to))

        def arrival(s):
            frm = lax.rem(w + M - s, M)
            return remote(src.at[frm], dst.at[frm], ssem.at[s - 1], rsem.at[s - 1], member(lax.rem(w + s, M)))

        def start():
            for s in range(1, M):
                copy(s).start()
            dst[w] = src[w]

        def wait():
            for s in range(1, M):
                copy(s).wait_send()
                arrival(s).wait_recv()

        return start, wait

    g_start, g_wait = to_members(gsend, grecv, gs, gr)
    o_start, o_wait = to_members(oret, orecv, os_, or_)
    s_start, s_wait = to_members(ssend, srecv, ss, sr)
    r_start, r_wait = to_members(gret, gback, rs, rr)
    g_start()
    cross_start(1)

    for a in (K, Q, V, G):
        for p in range(4):
            x = xin[a, p]
            xt[a, p] = (x * 0.125).T if a == Q else x.T

    causal = iota((B, B), 0) <= iota((B, B), 1)

    def softmax_block(s, i):
        n = s.shape[0]
        chunks = [s[b * B : (b + 1) * B] for b in range(n // B)]
        if i is not None:
            chunks[-1] = jnp.where(causal, chunks[-1], NEG)
        m = jnp.max(chunks[0], axis=0, keepdims=True)
        for x in chunks[1:]:
            m = jnp.maximum(m, jnp.max(x, axis=0, keepdims=True))
        total = None
        parts = []
        for x in chunks:
            x = jnp.exp(x - m)
            t = jnp.sum(x, axis=0, keepdims=True)
            total = t if total is None else total + t
            parts.append(x.astype(BF))
        return m, total, parts

    def join(parts):
        return parts[0] if len(parts) == 1 else jnp.concatenate(parts, axis=0)

    def place_one(kb, i):
        if kb == 0:
            return 0, i * B
        return B, (i - 1) * B if kb == 1 else 2 * B

    def one_block(hh, kb, i):
        r, l = place_one(kb, i)
        return pst.at[hh, r : r + B, l : l + B]

    def one_tail(hh, kb):
        r, l = place_one(kb, kb)
        return pst[hh, r : r + B, l : l + (NB - kb) * B]

    def forward_one(p):
        for i in range(NB):
            n = (i + 1) * B
            for e in (0, 1):
                hh = 2 * p + e
                s = dot(xin[K, p, :n], half_rows(xt[Q, p, :, i * B : n], e))
                m, total, parts = softmax_block(s, i)
                for kb in range(i + 1):
                    one_block(hh, kb, i)[...] = parts[kb]
                o1[hh * HD : (hh + 1) * HD, i * B : n] = dot(xt[V, p, e * HD : (e + 1) * HD, :n], join(parts))
                st1[hh : hh + 1, i * B : n] = m
                st1[8 + hh : 9 + hh, i * B : n] = total

    for p in range(4):
        forward_one(p)

    scale = jnp.where(late == 0, 0.125, 1.0).astype(F32)
    kv_slot = jnp.where(late == 0, 2, 4)
    qg_slot = jnp.where(late == 0, 4, 0)

    def xo_copy(p):
        return remote(xo.at[0, p], xo.at[1, p], xos.at[p], xor_.at[p], far)

    def forward_cross(p):
        kv, qg = kv_slot + p, qg_slot + p
        for i in range(NB):
            at = slice(i * B, (i + 1) * B)
            for e in (0, 1):
                hh = 2 * p + e
                m, total, parts = softmax_block(dot(xin[K, kv], half_rows(xt[Q, qg, :, at], e)), None)
                wts = join(parts)
                pc[hh, :, at] = wts
                ox[hh * HD : (hh + 1) * HD, at] = dot(xt[V, kv, e * HD : (e + 1) * HD, :], wts)
                stx[hh : hh + 1, at] = m
                stx[4 + hh : 5 + hh, at] = total
        logs = []
        for e in (0, 1):
            hh = 2 * p + e
            total = stx[4 + hh : 5 + hh]
            xo[0, p, e * HD : (e + 1) * HD] = (ox[hh * HD : (hh + 1) * HD] / total).astype(BF)
            logs += list(split3(stx[hh : hh + 1] + jnp.log(total)))
        xo[0, p, 128:144] = stack_rows(logs, 16).astype(BF)

        @pl.when(late == 0)
        def _():
            xo_copy(p).start()
            xo[1, p] = jnp.zeros(xo.shape[2:], BF)

    cross_wait(0)
    for a, slot in ((late, 4), (2 * late, 5 - late)):
        xt[a, slot] = (xin[a, slot].astype(F32) * scale).astype(BF).T
    forward_cross(0)

    g_wait()
    for i in range(M):
        mqk[i * MR : (i + 1) * MR] = grecv[i, :MR, :128]
        mvg[i * MR : (i + 1) * MR] = grecv[i, :MR, 128:]
        tqk[i * 32 : (i + 1) * 32] = grecv[i, MR:, :128]
        tvg[i * 32 : (i + 1) * 32] = grecv[i, MR:, 128:]
    ttkv[group] = jnp.where(iota((TQ, 128), 1) < HD, tvg[...], tqk[...])

    def top_copy(s):
        return remote(ttkv.at[group], ttkv.at[group], ts.at[s - 1], tr.at[s - 1], at_group(lax.rem(group + s, groups)))

    def top_arrival(s):
        frm = lax.rem(group + groups - s, groups)
        return remote(ttkv.at[frm], ttkv.at[frm], ts.at[s - 1], tr.at[s - 1], at_group(lax.rem(group + s, groups)))

    for s in range(1, groups):
        @pl.when(group + s < groups)
        def _():
            top_copy(s).start()

    def clear(g, carry):
        ttkv[g] = jnp.zeros((TQ, 128), BF)
        return carry

    lax.fori_loop(group + 1, groups, clear, 0)

    def place_mid(kb, i):
        if kb < MB // 2:
            return kb * B, (i - kb) * B
        return (MB - 1 - kb) * B, (i + 1) * B

    def mid_block(kb, i):
        r, l = place_mid(kb, i)
        return pm.at[r : r + B, l : l + B]

    def mid_tail(kb):
        r, l = place_mid(kb, kb)
        return pm[r : r + B, l : l + (MB - kb) * B]

    mqk_t[...] = mqk[...].T
    mvg_t[...] = mvg[...].T
    mq_w[...] = below(mqk_t[:HD] * 0.125)
    mg_w[...] = above(mvg_t[HD:])
    for i in range(MB):
        n = (i + 1) * B
        at = slice(i * B, n)
        m, total, parts = softmax_block(dot(mqk[:n], mq_w[:, at]), i)
        for kb in range(i + 1):
            mid_block(kb, i)[...] = parts[kb]
        om[:HD, at] = dot(mvg_t[:HD, :n], join(parts)) / total
        om[HD:, at] = stack_rows(split3(m + jnp.log(total)), HD)
        stm[0:1, at] = m
        stm[1:2, at] = total
    x = om[...].astype(BF).T
    for i in range(M):
        oret[i, :MR] = x[i * MR : (i + 1) * MR]

    for s in range(1, groups):
        @pl.when(group + s < groups)
        def _():
            top_copy(s).wait_send()

        @pl.when(group >= s)
        def _():
            top_arrival(s).wait_recv()

    keys_n = groups * TQ
    kv_top = ttkv[...].reshape(keys_n, 128)
    ttkv_t[...] = kv_top.T
    tqk_t = tqk[...].T
    tq_w = below(tqk_t[:HD] * 0.125)
    tg_w = above(tvg[...].T[HD:])
    r = iota((keys_n, 1), 0)
    key_rank = jnp.where(
        (r & 31) < TR, (r >> 8) * (M * TR) + ((r >> 5) & 7) * TR + (r & 31), 1000000
    )
    r = iota((1, TQ), 1)
    query_rank = group * (M * TR) + (r >> 5) * TR + (r & 31)
    s = jnp.where(key_rank <= query_rank, dot(kv_top, tq_w), NEG)
    m, total, parts = softmax_block(s, None)
    x = join(parts)
    ptop[...] = x
    out = dot(ttkv_t[:HD], x) / total
    x = jnp.concatenate([out, stack_rows(split3(m + jnp.log(total)), HD)], axis=0).astype(BF).T
    for i in range(M):
        oret[i, MR:] = x[i * 32 : (i + 1) * 32]
    stt[0:1] = total
    o_start()

    cross_wait(1)
    for a, slot in ((3 - 2 * late, 4 + late), (3 - late, 5)):
        xt[a, slot] = xin[a, slot].T
    forward_cross(1)

    o_wait()
    lane_mid = iota((80, CR), 1) < MR

    def out_copy(a, p):
        i = a * 4 + p
        return remote(ostage.at[a, p, theirs], outs[a].at[:, lanes(core, p)], fs.at[i], fr.at[i], mate)

    def out_arrival(a, p):
        i = a * 4 + p
        return remote(ostage.at[a, p, theirs], outs[a].at[:, lanes(1 - core, p)], fs.at[i], fr.at[i], mate)

    def out_local(a, p):
        return pltpu.make_async_copy(ostage.at[a, p, mine], outs[a].at[:, lanes(core, p)], fl.at[a * 4 + p])

    def out_start(a, p):
        out_copy(a, p).start()
        out_local(a, p).start()

    for hh in range(8):
        p, e = hh // 2, hh % 2
        rows = slice(hh * HD, (hh + 1) * HD)
        if p >= 2 and e == 0:
            @pl.when(late == 0)
            def _():
                xo_copy(p - 2).wait_send()

            @pl.when(late == 1)
            def _():
                xo_copy(p - 2).wait_recv()

        x = orecv[hh].T[:80]
        x = jnp.concatenate([keep(x, lane_mid), keep(x, ~lane_mid)], axis=0)
        x = dot(x, ehot[hh])
        out_m, out_t = x[:HD], x[80 : 80 + HD]
        log_m = x[64:65] + x[65:66] + x[66:67]
        log_t = x[144:145] + x[145:146] + x[146:147]
        log_m = jnp.where((token & (MIDDLE - 1)) == off_mid[hh], log_m, NEG)
        log_t = jnp.where((token & (C - 1)) == off_top[hh], log_t, NEG)
        j = hh % 4
        out_x = xo[hh // 4, p % 2, e * HD : (e + 1) * HD].astype(F32)
        x = xo[hh // 4, p % 2, 128:144].astype(F32)
        log_x = x[3 * e : 3 * e + 1] + x[3 * e + 1 : 3 * e + 2] + x[3 * e + 2 : 3 * e + 3]
        log_x = jnp.where(late == 1, log_x, NEG)
        total = st1[8 + hh : 9 + hh]
        log_1 = st1[hh : hh + 1] + jnp.log(total)
        peak = jnp.maximum(jnp.maximum(log_1, log_x), jnp.maximum(log_m, log_t))
        e_1, e_x = jnp.exp(log_1 - peak), jnp.exp(log_x - peak)
        e_m, e_t = jnp.exp(log_m - peak), jnp.exp(log_t - peak)
        norm = e_1 + e_x + e_m + e_t
        s_x, s_m, s_t = e_x / norm, e_m / norm, e_t / norm
        c_1 = e_1 / norm / total
        mixed = c_1 * o1[rows] + s_x * out_x + s_m * out_m + s_t * out_t
        o1[rows] = mixed
        delta = jnp.sum(xt[G, p, e * HD : (e + 1) * HD].astype(F32) * mixed, axis=0, keepdims=True)
        cd1[hh : hh + 1] = c_1
        cd1[8 + hh : 9 + hh] = delta
        stats = stack_rows(split3(s_m) + split3(s_t) + split3(delta), 16).astype(BF)
        g = dot(stats, ehot_t[hh])
        share = jnp.where(lane_first, g[0:1] + g[1:2] + g[2:3], g[3:4] + g[4:5] + g[5:6])
        ssend[hh, :, :CR] = stack_rows((share, g[6:7] + g[7:8] + g[8:9]), 8)
        if hh < 4:
            @pl.when(late == 1)
            def _():
                sx_in[j : j + 1] = s_x
                sx_in[4 + j : 5 + j] = delta
        else:
            sx_out[j : j + 1] = s_x
            sx_out[4 + j : 5 + j] = delta
        if e == 1:
            ostage[0, p] = o1[p * 128 : (p + 1) * 128].astype(BF).T
            out_start(0, p)

    sx_copy = remote(sx_out, sx_in, sxs.at[0], sxr.at[0], far)

    @pl.when(late == 1)
    def _():
        sx_copy.start()

    s_start()

    def scaled(x, c_low, c_high):
        return (x.astype(F32) * jnp.where(iota(x.shape, 0) < HD, c_low, c_high)).astype(BF).T

    def backward_one(p):
        cs = (cd1[2 * p : 2 * p + 1], cd1[2 * p + 1 : 2 * p + 2])
        gc, qc = scaled(xt[G, p], *cs), scaled(xt[Q, p], *cs)
        gcs = [half_lanes(gc, e) for e in (0, 1)]
        qcs = [half_lanes(qc, e) for e in (0, 1)]
        for kb in range(NB):
            dv[p, kb * B : (kb + 1) * B] = dot(one_tail(2 * p, kb), gcs[0][kb * B :]) + dot(
                one_tail(2 * p + 1, kb), gcs[1][kb * B :]
            )
        for i in range(NB):
            n = (i + 1) * B
            for e in (0, 1):
                hh = 2 * p + e
                dp = dot(xin[V, p, :n], half_rows(xt[G, p, :, i * B : n], e))
                delta = cd1[8 + hh : 9 + hh, i * B : n]
                parts = []
                for kb in range(i + 1):
                    x = one_block(hh, kb, i)[...].astype(F32)
                    x = (x * (dp[kb * B : (kb + 1) * B] - delta)).astype(BF)
                    one_block(hh, kb, i)[...] = x
                    parts.append(x)
                dqt[hh * HD : (hh + 1) * HD, i * B : n] = dot(
                    xt[K, p, e * HD : (e + 1) * HD, :n], join(parts)
                ) * (cs[e][:, i * B : n] * 0.125)
        for kb in range(NB):
            dk[p, kb * B : (kb + 1) * B] = dot(one_tail(2 * p, kb), qcs[0][kb * B :]) + dot(
                one_tail(2 * p + 1, kb), qcs[1][kb * B :]
            )

    backward_one(0)

    @pl.when(late == 1)
    def _():
        sx_copy.wait_send()

    @pl.when(late == 0)
    def _():
        sx_copy.wait_recv()

    xdq_copy = remote(xdq.at[0], xdq.at[1], xds.at[4], xdr.at[4], far)

    def xdkv_copy(n, p):
        i = n * 2 + p
        return remote(xdkv.at[0, n, p], xdkv.at[1, n, p], xds.at[i], xdr.at[i], far)

    for p in (0, 1):
        kv, qg = kv_slot + p, qg_slot + p
        cs = [sx_in[2 * p + e : 2 * p + e + 1] / stx[4 + 2 * p + e : 5 + 2 * p + e] for e in (0, 1)]
        gc, qc = scaled(xt[G, qg], *cs), scaled(xt[Q, qg], *cs)
        xdkv[0, 1, p] = (dot(pc[2 * p], half_lanes(gc, 0)) + dot(pc[2 * p + 1], half_lanes(gc, 1))).astype(BF)

        @pl.when(late == 1)
        def _():
            xdkv_copy(1, p).start()

        for i in range(NB):
            at = slice(i * B, (i + 1) * B)
            for e in (0, 1):
                hh = 2 * p + e
                dp = dot(xin[V, kv], half_rows(xt[G, qg, :, at], e))
                x = (pc[hh, :, at].astype(F32) * (dp - sx_in[4 + hh : 5 + hh, at])).astype(BF)
                pc[hh, :, at] = x
                x = dot(xt[K, kv, e * HD : (e + 1) * HD, :], x) * (cs[e][:, at] * 0.125)
                xdq[0, hh * HD : (hh + 1) * HD, at] = x.astype(BF)
        xdkv[0, 0, p] = (dot(pc[2 * p], half_lanes(qc, 0)) + dot(pc[2 * p + 1], half_lanes(qc, 1))).astype(BF)

        @pl.when(late == 1)
        def _():
            xdkv_copy(0, p).start()

    @pl.when(late == 0)
    def _():
        xdq_copy.start()

    s_wait()
    t_stats = jnp.concatenate([srecv[i, :, MR:CR] for i in range(M)], axis=1)
    m_stats = jnp.concatenate([srecv[i, :, :MR] for i in range(M)], axis=1)
    t_c = t_stats[0:1] / stt[0:1]
    kv_top = ttkv[...].reshape(keys_n, 128)
    dp = dot(kv_top, tg_w)
    ds = (ptop[...].astype(F32) * (dp - t_stats[1:2])).astype(BF)
    t_dq = above(dot(ttkv_t[HD:], ds) * (t_c * 0.125)).astype(BF).T
    gc = above((tg_w[:HD].astype(F32) * t_c).astype(BF)).T
    qc = below((tq_w[HD:].astype(F32) * t_c).astype(BF)).T
    tpart[...] = (dot(ptop[...], gc) + dot(ds, qc)).astype(BF).reshape(groups, TQ, 128)

    def part_copy(s):
        to = lax.rem(group + groups - s, groups)
        return remote(tpart.at[to], trec.at[group], tps.at[s - 1], tpr.at[s - 1], at_group(to))

    def part_arrival(s):
        frm = lax.rem(group + s, groups)
        return remote(tpart.at[frm], trec.at[frm], tps.at[s - 1], tpr.at[s - 1], at_group(lax.rem(group + groups - s, groups)))

    for s in range(1, groups):
        @pl.when(group >= s)
        def _():
            part_copy(s).start()

    m_c = m_stats[0:1] / stm[1:2]
    gc = above((mg_w[:HD].astype(F32) * m_c).astype(BF)).T
    qc = below((mq_w[HD:].astype(F32) * m_c).astype(BF)).T
    m_dv = [dot(mid_tail(kb), gc[kb * B :]) for kb in range(MB)]
    for i in range(MB):
        n = (i + 1) * B
        at = slice(i * B, n)
        dp = dot(mvg[:n], mg_w[:, at])
        parts = []
        for kb in range(i + 1):
            x = mid_block(kb, i)[...].astype(F32)
            x = (x * (dp[kb * B : (kb + 1) * B] - m_stats[1:2, at])).astype(BF)
            mid_block(kb, i)[...] = x
            parts.append(x)
        dqm[:, at] = dot(mqk_t[HD:, :n], join(parts)) * (m_c[:, at] * 0.125)
    m_vk = [m_dv[kb] + dot(mid_tail(kb), qc[kb * B :]) for kb in range(MB)]
    m_vk = jnp.concatenate(m_vk, axis=0).astype(BF)
    m_dq = above(dqm[...]).astype(BF).T
    for i in range(M):
        gret[i, :MR, :128] = m_vk[i * MR : (i + 1) * MR]
        gret[i, :MR, 128:] = m_dq[i * MR : (i + 1) * MR]
        gret[i, MR:, 128:] = t_dq[i * 32 : (i + 1) * 32]
    for s in range(1, groups):
        @pl.when(group >= s)
        def _():
            part_copy(s).wait_send()

        @pl.when(group + s < groups)
        def _():
            part_arrival(s).wait_recv()

    def add_part(g, x):
        return x + trec[g].astype(F32)

    x = lax.fori_loop(group + 1, groups, add_part, tpart[group].astype(F32)).astype(BF)
    for i in range(M):
        gret[i, MR:, :128] = x[i * 32 : (i + 1) * 32]
    r_start()

    backward_one(1)
    backward_one(2)
    backward_one(3)

    @pl.when(late == 0)
    def _():
        xdq_copy.wait_send()
        for n in (0, 1):
            for p in (0, 1):
                xdkv_copy(n, p).wait_recv()

    @pl.when(late == 1)
    def _():
        xdq_copy.wait_recv()
        for n in (0, 1):
            for p in (0, 1):
                xdkv_copy(n, p).wait_send()

    r_wait()
    for p in range(4):
        rows = slice(p * 128, (p + 1) * 128)

        @pl.when(late == 1)
        def _():
            dqt[rows] += xdq[p // 2, (p % 2) * 128 : (p % 2 + 1) * 128].astype(F32)

        @pl.when(late == 0)
        def _():
            dk[p] += xdkv[1 - p // 2, 0, p % 2].astype(F32)
            dv[p] += xdkv[1 - p // 2, 1, p % 2].astype(F32)

        sums = None
        for e in (0, 1):
            y = gback[2 * p + e]
            vk, yq = y[:, :128], y[:, 128:]
            turned = swap_halves(vk).astype(BF)
            if e == 0:
                y = (half_lanes(vk, 0), half_lanes(turned, 0), yq)
            else:
                y = (half_lanes(turned, 1), half_lanes(vk, 1), swap_halves(yq).astype(BF))
            t = dot(ehot_t[2 * p + e], jnp.concatenate(y, axis=1))
            sums = t if sums is None else sums + t
        ostage[1, p] = (dqt[rows].T + sums[:, 256:]).astype(BF)
        ostage[2, p] = (dk[p] + sums[:, 128:256]).astype(BF)
        ostage[3, p] = (dv[p] + sums[:, :128]).astype(BF)
        for a in (1, 2, 3):
            out_start(a, p)

    for a in range(4):
        for p in range(4):
            out_local(a, p).wait()
            out_copy(a, p).wait_send()
            out_arrival(a, p).wait_recv()


def hand_over(*refs):
    sources, results, (held, in_sem, out_sem) = refs[:4], refs[4:8], refs[8:]
    reads = [pltpu.make_async_copy(sources[i], held.at[i], in_sem.at[i]) for i in range(4)]
    writes = [pltpu.make_async_copy(held.at[i], results[i], out_sem.at[i]) for i in range(4)]
    for copy in reads:
        copy.start()
    for read, write in zip(reads, writes):
        read.wait()
        write.start()
    for copy in writes:
        copy.wait()


def solution(mesh):
    C = mesh.shape["ctx"]

    def shards(queries, keys, values, grad_out, offset_mid, head_top_offsets):
        T, W = queries.shape
        N = 2 * T
        CR = N // MIDDLE + 32
        R = 8 * (N // MIDDLE)
        TK = C // MIDDLE * 256
        shape = jax.ShapeDtypeStruct((T, W), BF)
        hbm = pl.BlockSpec(memory_space=pl.ANY)
        smem = pl.BlockSpec(memory_space=pltpu.SMEM)
        vm = pltpu.VMEM
        dma = pltpu.SemaphoreType.DMA
        scratch = [
            vm((8, 128), jnp.int32),
            vm((4, 8, 128), jnp.int32),
            vm((4, 6, N, 128), BF),
            vm((4, 6, 128, N), BF),
            vm((8, 2 * B, N), BF),
            vm((4, N, N), BF),
            vm((R // 2, R + B), BF),
            vm((TK, 256), BF),
            vm((8, CR, N), BF),
            vm((8, N, CR), BF),
            vm((8, CR, 256), BF),
            vm((8, CR, 256), BF),
            vm((R, 128), BF),
            vm((R, 128), BF),
            vm((128, R), BF),
            vm((128, R), BF),
            vm((128, R), BF),
            vm((128, R), BF),
            vm((256, 128), BF),
            vm((256, 128), BF),
            vm((C // MIDDLE, 256, 128), BF),
            vm((128, TK), BF),
            vm((512, N), F32),
            vm((256, N), F32),
            vm((16, N), F32),
            vm((8, N), F32),
            vm((8, R), F32),
            vm((8, 256), F32),
            vm((16, N), F32),
            vm((2, 2, 144, N), BF),
            vm((8, N), F32),
            vm((8, N), F32),
            vm((128, R), F32),
            vm((8, CR, 128), BF),
            vm((8, CR, 128), BF),
            vm((8, 8, 256), F32),
            vm((8, 8, 256), F32),
            vm((512, N), F32),
            vm((4, N, 128), F32),
            vm((4, N, 128), F32),
            vm((2, 256, N), BF),
            vm((2, 2, 2, N, 128), BF),
            vm((HD, R), F32),
            vm((8, CR, 256), BF),
            vm((8, CR, 256), BF),
            vm((C // MIDDLE, 256, 128), BF),
            vm((C // MIDDLE, 256, 128), BF),
            vm((4, 4, N, 128), BF),
            dma((3,)), dma((3,)), dma((16,)), dma((16,)), dma((16,)),
            dma((8,)), dma((8,)), dma((7,)), dma((7,)), dma((7,)), dma((7,)),
            dma((7,)), dma((7,)), dma((2,)), dma((2,)), dma((7,)), dma((7,)),
            dma((1,)), dma((1,)), dma((7,)), dma((7,)), dma((7,)), dma((7,)),
            dma((5,)), dma((5,)), dma((16,)), dma((16,)), dma((16,)),
        ]
        results = pl.pallas_call(
            functools.partial(kernel, C, T),
            out_shape=[shape] * 4,
            in_specs=[smem, smem, hbm, hbm, hbm, hbm],
            out_specs=[hbm] * 4,
            scratch_shapes=scratch,
            compiler_params=pltpu.CompilerParams(
                collective_id=0, has_side_effects=True, vmem_limit_bytes=62 << 20
            ),
            name="attention",
        )(offset_mid, head_top_offsets, queries, keys, values, grad_out)
        return pl.pallas_call(
            hand_over,
            out_shape=[shape] * 4,
            in_specs=[hbm] * 4,
            out_specs=[hbm] * 4,
            scratch_shapes=[vm((4, T, W), BF), dma((4,)), dma((4,))],
            compiler_params=pltpu.CompilerParams(vmem_limit_bytes=62 << 20),
            name="hand_over",
        )(*results)

    rows = P(("ctx", "head"), None)
    return jax.shard_map(
        shards,
        mesh=mesh,
        in_specs=(rows, rows, rows, rows, P("head"), P("head")),
        out_specs=(rows,) * 4,
        check_vma=False,
    )
```

```python
import functools

import jax
import jax.numpy as jnp
from jax import lax
from jax.experimental import pallas as pl
from jax.experimental.pallas import tpu as pltpu
from jax.sharding import PartitionSpec as P

MESH = pl.DeviceIdType.MESH
HD = 64
MIDDLE = 4
B = 256
NEG = -1e30
F32 = jnp.float32
BF = jnp.bfloat16
Q, K, V, G = 0, 1, 2, 3


def dot(a, b):
    return jnp.dot(a, b, preferred_element_type=F32)


def iota(shape, dim):
    return lax.broadcasted_iota(jnp.int32, shape, dim)


def keep(x, mask):
    return jnp.where(mask, x, jnp.zeros_like(x))


def half_rows(x, e):
    return keep(x, (iota(x.shape, 0) >= HD) == (e == 1))


def half_lanes(x, e):
    return keep(x, (iota(x.shape, 1) >= HD) == (e == 1))


def swap_halves(x):
    return pltpu.roll(x.astype(F32), HD, 1)


def split3(x):
    hi = x.astype(BF).astype(F32)
    rest = x - hi
    mid = rest.astype(BF).astype(F32)
    return hi, mid, rest - mid


def stack_rows(rows, count):
    n = rows[0].shape[1]
    at = iota((count, n), 0)
    out = jnp.zeros((count, n), F32)
    for i, row in enumerate(rows):
        out = jnp.where(at == i, row, out)
    return out


def above(x):
    return jnp.concatenate([x, jnp.zeros_like(x)], axis=0)


def below(x):
    return jnp.concatenate([jnp.zeros_like(x), x], axis=0)


def pack_halves(x, n):
    pieces = [x[:, i : i + n] for i in range(0, x.shape[1], n)]
    return jnp.concatenate(
        [jnp.concatenate(pieces[0::2], axis=1), jnp.concatenate(pieces[1::2], axis=1)], axis=0
    )


def kernel(
    C, T,
    mid_in, top_in, q_in, k_in, v_in, g_in,
    o_out, dq_out, dk_out, dv_out,
    off_in, offs, xin, xt, pst, pc, pm, ptop, ehot, ehot_t,
    gsend, grecv, mqk, mvg, mqk_t, mvg_t, mq_w, mg_w, tqk, tvg, ttkv, ttkv_t,
    o1, ox, st1, stx, stm, stt, cd1, xo, sx_in, sx_out, om, oret, orecv, ssend, srecv,
    dqt, dk, dv, xdq, xdkv, dqm, gret, gback, tpart, trec, ostage,
    off_s, off_r, sw_s, sw_r, sw_l, xs, xr, gs, gr, ts, tr, os_, or_, xos, xor_,
    ss, sr, sxs, sxr, tps, tpr, rs, rr, xds, xdr, fs, fr, fl,
):
    N = 2 * T
    NB = N // B
    M = 8
    MR = N // MIDDLE
    TR = N // C
    CR = MR + 32
    R = M * MR
    MB = R // B
    TQ = M * 32
    c = lax.axis_index("ctx")
    h = lax.axis_index("head")
    core = lax.rem(h, 2)
    late = h // 2
    group = c // MIDDLE
    w = lax.rem(c, MIDDLE) * 2 + late
    groups = C // MIDDLE
    ins = (q_in, k_in, v_in, g_in)
    outs = (o_out, dq_out, dk_out, dv_out)
    mate = (c, h + 1 - 2 * core)
    far = (c, lax.rem(h + 2, 4))
    across = (c, 3 - h)

    def member(i):
        return (group * MIDDLE + i // 2, 2 * lax.rem(i, 2) + core)

    def at_group(g):
        return (g * MIDDLE + lax.rem(c, MIDDLE), h)

    bar = pltpu.get_barrier_semaphore()

    def greet(dev):
        pl.semaphore_signal(bar, inc=1, device_id=dev, device_id_type=MESH)

    greet(mate)
    greet(across)
    for s in range(1, M):
        greet(member(lax.rem(w + s, M)))
    for s in range(1, groups):
        greet(at_group(lax.rem(group + s, groups)))

    def lanes(of, p):
        return pl.ds(pl.multiple_of(of * 512 + p * 128, 128), 128)

    mine = pl.ds(pl.multiple_of(core * T, T), T)
    theirs = pl.ds(pl.multiple_of((1 - core) * T, T), T)

    def swap_local(a, p):
        return pltpu.make_async_copy(ins[a].at[:, lanes(core, p)], xin.at[a, p, mine], sw_l.at[a * 4 + p])

    for a in (K, Q, V, G):
        for p in range(4):
            swap_local(a, p).start()
    for j in range(4):
        off_in[j : j + 1] = jnp.full((1, 128), mid_in[j], jnp.int32)
        off_in[4 + j : 5 + j] = jnp.full((1, 128), top_in[j], jnp.int32)
    offs[h] = off_in[...]
    pl.semaphore_wait(bar, 2 + M - 1 + groups - 1)

    def remote(src, dst, ssem, rsem, dev):
        return pltpu.make_async_remote_copy(
            src_ref=src, dst_ref=dst, send_sem=ssem, recv_sem=rsem,
            device_id=dev, device_id_type=MESH,
        )

    def off_copy(s):
        to = lax.rem(h + s, 4)
        return remote(off_in, offs.at[h], off_s.at[s - 1], off_r.at[s - 1], (c, to))

    def off_arrival(s):
        frm = lax.rem(h + 4 - s, 4)
        return remote(off_in, offs.at[frm], off_s.at[s - 1], off_r.at[s - 1], (c, lax.rem(h + s, 4)))

    for s in (1, 2, 3):
        off_copy(s).start()

    def swap_copy(a, p):
        i = a * 4 + p
        return remote(ins[a].at[:, lanes(1 - core, p)], xin.at[a, p, mine], sw_s.at[i], sw_r.at[i], mate)

    def swap_arrival(a, p):
        i = a * 4 + p
        return remote(ins[a].at[:, lanes(1 - core, p)], xin.at[a, p, theirs], sw_s.at[i], sw_r.at[i], mate)

    for a in (K, Q, V, G):
        for p in range(4):
            swap_copy(a, p).start()

    waves = (
        (((K, 0), (V, 0)), ((Q, 0), (Q, 1))),
        (((K, 1), (V, 1)), ((G, 0), (G, 1))),
    )

    def cross_copy(wave, n, a, p, side):
        i = wave * 4 + n * 2 + side
        pair = p if a in (K, V) else 2 + p
        of = core if side == 0 else 1 - core
        return remote(
            ins[a].at[:, lanes(of, pair)], xin.at[a, 4 + p, mine], xs.at[i], xr.at[i],
            far if side == 0 else across,
        )

    def cross_arrival(wave, n, a, p, side):
        i = wave * 4 + n * 2 + side
        return remote(
            ins[a].at[:, lanes(core, p)], xin.at[a, 4 + p, mine if side == 0 else theirs],
            xs.at[i], xr.at[i], far if side == 0 else across,
        )

    def cross_start(wave):
        for half in (0, 1):
            @pl.when(late == half)
            def _():
                for n, (a, p) in enumerate(waves[wave][half]):
                    for side in (0, 1):
                        cross_copy(wave, n, a, p, side).start()

    def cross_wait(wave, half):
        for side in (0, 1):
            for n, (a, p) in enumerate(waves[wave][half]):
                cross_copy(wave, n, a, p, side).wait_send()
            for n, (a, p) in enumerate(waves[wave][1 - half]):
                cross_arrival(wave, n, a, p, side).wait_recv()

    cross_start(0)

    for s in (1, 2, 3):
        off_copy(s).wait_send()
        off_arrival(s).wait_recv()
    r = iota((CR, N), 0)
    first = r < MR
    row_from = iota((CR, N), 1) - jnp.where(
        first, MIDDLE * r, jnp.where(r < MR + TR, C * (r - MR), -1000000)
    )
    r = iota((1, CR), 1)
    lane_first = r < MR
    lane_to = jnp.where(lane_first, MIDDLE * r, jnp.where(r < MR + TR, C * (r - MR), -1000000))
    token_row = iota((N, CR), 0)
    token = iota((1, N), 1)
    off_mid, off_top = [], []
    for hd in range(8):
        of = 2 * core + hd // 4
        j = hd % 4
        mid_row = offs[of, j : j + 1, :]
        top_row = offs[of, 4 + j : 5 + j, :]
        mid_n = jnp.concatenate([mid_row] * (N // 128), axis=1)
        top_n = jnp.concatenate([top_row] * (N // 128), axis=1)
        off_mid.append(mid_n)
        off_top.append(top_n)
        ehot[hd] = (row_from == jnp.where(first, mid_n, top_n)).astype(F32).astype(BF)
        goal = lane_to + jnp.where(lane_first, mid_n[:, :CR], top_n[:, :CR])
        ehot_t[hd] = (token_row == goal).astype(F32).astype(BF)

    for a in (K, Q, V, G):
        for p in range(4):
            swap_local(a, p).wait()
            swap_copy(a, p).wait_send()
            swap_arrival(a, p).wait_recv()

    low = iota((CR, 128), 1) < HD
    for p in range(4):
        for n, (a, b) in enumerate(((Q, K), (V, G))):
            x = jnp.concatenate([xin[a, p], xin[b, p]], axis=1)
            for e in (0, 1):
                t = dot(ehot[2 * p + e], x)
                if e == 0:
                    t = jnp.where(low, t[:, :128], swap_halves(t[:, 128:]))
                else:
                    t = jnp.where(low, swap_halves(t[:, :128]), t[:, 128:])
                gsend[2 * p + e, :, n * 128 : (n + 1) * 128] = t.astype(BF)

    def to_members(src, dst, ssem, rsem):
        def copy(s):
            to = lax.rem(w + s, M)
            return remote(src.at[to], dst.at[w], ssem.at[s - 1], rsem.at[s - 1], member(to))

        def arrival(s):
            frm = lax.rem(w + M - s, M)
            return remote(src.at[frm], dst.at[frm], ssem.at[s - 1], rsem.at[s - 1], member(lax.rem(w + s, M)))

        def start():
            for s in range(1, M):
                copy(s).start()
            dst[w] = src[w]

        def wait():
            for s in range(1, M):
                copy(s).wait_send()
                arrival(s).wait_recv()

        return start, wait

    g_start, g_wait = to_members(gsend, grecv, gs, gr)
    o_start, o_wait = to_members(oret, orecv, os_, or_)
    s_start, s_wait = to_members(ssend, srecv, ss, sr)
    r_start, r_wait = to_members(gret, gback, rs, rr)
    g_start()
    cross_start(1)

    for a in (K, Q, V, G):
        for p in range(4):
            x = xin[a, p]
            xt[a, p] = (x * 0.125).T if a == Q else x.T

    causal = iota((B, B), 0) <= iota((B, B), 1)

    def softmax_block(s, i):
        n = s.shape[0]
        chunks = [s[b * B : (b + 1) * B] for b in range(n // B)]
        if i is not None:
            chunks[-1] = jnp.where(causal, chunks[-1], NEG)
        m = jnp.max(chunks[0], axis=0, keepdims=True)
        for x in chunks[1:]:
            m = jnp.maximum(m, jnp.max(x, axis=0, keepdims=True))
        total = None
        parts = []
        for x in chunks:
            x = jnp.exp(x - m)
            t = jnp.sum(x, axis=0, keepdims=True)
            total = t if total is None else total + t
            parts.append(x.astype(BF))
        return m, total, parts

    def join(parts):
        return parts[0] if len(parts) == 1 else jnp.concatenate(parts, axis=0)

    def place_one(kb, i):
        if kb == 0:
            return 0, i * B
        return B, (i - 1) * B if kb == 1 else 2 * B

    def one_block(hh, kb, i):
        r, l = place_one(kb, i)
        return pst.at[hh, r : r + B, l : l + B]

    def one_tail(hh, kb):
        r, l = place_one(kb, kb)
        return pst[hh, r : r + B, l : l + (NB - kb) * B]

    def forward_one(p):
        for i in range(NB):
            n = (i + 1) * B
            for e in (0, 1):
                hh = 2 * p + e
                s = dot(xin[K, p, :n], half_rows(xt[Q, p, :, i * B : n], e))
                m, total, parts = softmax_block(s, i)
                for kb in range(i + 1):
                    one_block(hh, kb, i)[...] = parts[kb]
                o1[hh * HD : (hh + 1) * HD, i * B : n] = dot(xt[V, p, e * HD : (e + 1) * HD, :n], join(parts))
                st1[hh : hh + 1, i * B : n] = m
                st1[8 + hh : 9 + hh, i * B : n] = total

    for p in range(4):
        forward_one(p)

    scale = jnp.where(late == 0, 0.125, 1.0).astype(F32)
    kv_slot = jnp.where(late == 0, 2, 4)
    qg_slot = jnp.where(late == 0, 4, 0)

    def xo_copy(p):
        return remote(xo.at[0, p], xo.at[1, p], xos.at[p], xor_.at[p], far)

    def forward_cross(p):
        kv, qg = kv_slot + p, qg_slot + p
        for i in range(NB):
            at = slice(i * B, (i + 1) * B)
            for e in (0, 1):
                hh = 2 * p + e
                m, total, parts = softmax_block(dot(xin[K, kv], half_rows(xt[Q, qg, :, at], e)), None)
                wts = join(parts)
                pc[hh, :, at] = wts
                ox[hh * HD : (hh + 1) * HD, at] = dot(xt[V, kv, e * HD : (e + 1) * HD, :], wts)
                stx[hh : hh + 1, at] = m
                stx[4 + hh : 5 + hh, at] = total
        logs = []
        for e in (0, 1):
            hh = 2 * p + e
            total = stx[4 + hh : 5 + hh]
            xo[0, p, e * HD : (e + 1) * HD] = (ox[hh * HD : (hh + 1) * HD] / total).astype(BF)
            logs += list(split3(stx[hh : hh + 1] + jnp.log(total)))
        xo[0, p, 128:144] = stack_rows(logs, 16).astype(BF)

        @pl.when(late == 0)
        def _():
            xo_copy(p).start()
            xo[1, p] = jnp.zeros(xo.shape[2:], BF)

    for half in (0, 1):
        @pl.when(late == half)
        def _():
            cross_wait(0, half)

    for a, slot in ((late, 4), (2 * late, 5 - late)):
        xt[a, slot] = (xin[a, slot].astype(F32) * scale).astype(BF).T
    forward_cross(0)

    g_wait()
    for i in range(M):
        mqk[i * MR : (i + 1) * MR] = grecv[i, :MR, :128]
        mvg[i * MR : (i + 1) * MR] = grecv[i, :MR, 128:]
        tqk[i * 32 : (i + 1) * 32] = grecv[i, MR:, :128]
        tvg[i * 32 : (i + 1) * 32] = grecv[i, MR:, 128:]
    ttkv[group] = jnp.where(iota((TQ, 128), 1) < HD, tvg[...], tqk[...])

    def top_copy(s):
        return remote(ttkv.at[group], ttkv.at[group], ts.at[s - 1], tr.at[s - 1], at_group(lax.rem(group + s, groups)))

    def top_arrival(s):
        frm = lax.rem(group + groups - s, groups)
        return remote(ttkv.at[frm], ttkv.at[frm], ts.at[s - 1], tr.at[s - 1], at_group(lax.rem(group + s, groups)))

    for s in range(1, groups):
        @pl.when(group + s < groups)
        def _():
            top_copy(s).start()

    def clear(g, carry):
        ttkv[g] = jnp.zeros((TQ, 128), BF)
        return carry

    lax.fori_loop(group + 1, groups, clear, 0)

    def place_mid(kb, i):
        if kb < MB // 2:
            return kb * B, (i - kb) * B
        return (MB - 1 - kb) * B, (i + 1) * B

    def mid_block(kb, i):
        r, l = place_mid(kb, i)
        return pm.at[r : r + B, l : l + B]

    def mid_tail(kb):
        r, l = place_mid(kb, kb)
        return pm[r : r + B, l : l + (MB - kb) * B]

    mqk_t[...] = mqk[...].T
    mvg_t[...] = mvg[...].T
    mq_w[...] = below(mqk_t[:HD] * 0.125)
    mg_w[...] = above(mvg_t[HD:])
    for i in range(MB):
        n = (i + 1) * B
        at = slice(i * B, n)
        m, total, parts = softmax_block(dot(mqk[:n], mq_w[:, at]), i)
        for kb in range(i + 1):
            mid_block(kb, i)[...] = parts[kb]
        om[:HD, at] = dot(mvg_t[:HD, :n], join(parts)) / total
        om[HD:, at] = stack_rows(split3(m + jnp.log(total)), HD)
        stm[0:1, at] = m
        stm[1:2, at] = total
    x = om[...].astype(BF).T
    for i in range(M):
        oret[i, :MR] = x[i * MR : (i + 1) * MR]

    for s in range(1, groups):
        @pl.when(group + s < groups)
        def _():
            top_copy(s).wait_send()

        @pl.when(group >= s)
        def _():
            top_arrival(s).wait_recv()

    keys_n = groups * TQ
    kv_top = ttkv[...].reshape(keys_n, 128)
    ttkv_t[...] = kv_top.T
    tqk_t = tqk[...].T
    tq_w = below(tqk_t[:HD] * 0.125)
    tg_w = above(tvg[...].T[HD:])
    r = iota((keys_n, 1), 0)
    key_rank = jnp.where(
        (r & 31) < TR, (r >> 8) * (M * TR) + ((r >> 5) & 7) * TR + (r & 31), 1000000
    )
    r = iota((1, TQ), 1)
    query_rank = group * (M * TR) + (r >> 5) * TR + (r & 31)
    s = jnp.where(key_rank <= query_rank, dot(kv_top, tq_w), NEG)
    m, total, parts = softmax_block(s, None)
    x = join(parts)
    ptop[...] = x
    out = dot(ttkv_t[:HD], x) / total
    x = jnp.concatenate([out, stack_rows(split3(m + jnp.log(total)), HD)], axis=0).astype(BF).T
    for i in range(M):
        oret[i, MR:] = x[i * 32 : (i + 1) * 32]
    stt[0:1] = total
    o_start()

    @pl.when(late == 1)
    def _():
        cross_wait(1, 1)
        for a in (K, V):
            xt[a, 5] = xin[a, 5].T

    forward_cross(1)

    o_wait()
    lane_mid = iota((80, CR), 1) < MR

    def out_copy(a, p):
        i = a * 4 + p
        return remote(ostage.at[a, p, theirs], outs[a].at[:, lanes(core, p)], fs.at[i], fr.at[i], mate)

    def out_arrival(a, p):
        i = a * 4 + p
        return remote(ostage.at[a, p, theirs], outs[a].at[:, lanes(1 - core, p)], fs.at[i], fr.at[i], mate)

    def out_local(a, p):
        return pltpu.make_async_copy(ostage.at[a, p, mine], outs[a].at[:, lanes(core, p)], fl.at[a * 4 + p])

    def out_start(a, p):
        out_copy(a, p).start()
        out_local(a, p).start()

    for hh in range(8):
        p, e = hh // 2, hh % 2
        rows = slice(hh * HD, (hh + 1) * HD)
        if p >= 2 and e == 0:
            @pl.when(late == 0)
            def _():
                xo_copy(p - 2).wait_send()

            @pl.when(late == 1)
            def _():
                xo_copy(p - 2).wait_recv()

        x = orecv[hh].T[:80]
        x = jnp.concatenate([keep(x, lane_mid), keep(x, ~lane_mid)], axis=0)
        x = dot(x, ehot[hh])
        out_m, out_t = x[:HD], x[80 : 80 + HD]
        log_m = x[64:65] + x[65:66] + x[66:67]
        log_t = x[144:145] + x[145:146] + x[146:147]
        log_m = jnp.where((token & (MIDDLE - 1)) == off_mid[hh], log_m, NEG)
        log_t = jnp.where((token & (C - 1)) == off_top[hh], log_t, NEG)
        j = hh % 4
        out_x = xo[hh // 4, p % 2, e * HD : (e + 1) * HD].astype(F32)
        x = xo[hh // 4, p % 2, 128:144].astype(F32)
        log_x = x[3 * e : 3 * e + 1] + x[3 * e + 1 : 3 * e + 2] + x[3 * e + 2 : 3 * e + 3]
        log_x = jnp.where(late == 1, log_x, NEG)
        total = st1[8 + hh : 9 + hh]
        log_1 = st1[hh : hh + 1] + jnp.log(total)
        peak = jnp.maximum(jnp.maximum(log_1, log_x), jnp.maximum(log_m, log_t))
        e_1, e_x = jnp.exp(log_1 - peak), jnp.exp(log_x - peak)
        e_m, e_t = jnp.exp(log_m - peak), jnp.exp(log_t - peak)
        norm = e_1 + e_x + e_m + e_t
        s_x, s_m, s_t = e_x / norm, e_m / norm, e_t / norm
        c_1 = e_1 / norm / total
        mixed = c_1 * o1[rows] + s_x * out_x + s_m * out_m + s_t * out_t
        o1[rows] = mixed
        delta = jnp.sum(xt[G, p, e * HD : (e + 1) * HD].astype(F32) * mixed, axis=0, keepdims=True)
        cd1[hh : hh + 1] = c_1
        cd1[8 + hh : 9 + hh] = delta
        stats = stack_rows(split3(s_m) + split3(s_t) + split3(delta), 16).astype(BF)
        g = dot(stats, ehot_t[hh])
        share = jnp.where(lane_first, g[0:1] + g[1:2] + g[2:3], g[3:4] + g[4:5] + g[5:6])
        ssend[hh, :, :CR] = stack_rows((share, g[6:7] + g[7:8] + g[8:9]), 8)
        if hh < 4:
            @pl.when(late == 1)
            def _():
                sx_in[j : j + 1] = s_x
                sx_in[4 + j : 5 + j] = delta
        else:
            sx_out[j : j + 1] = s_x
            sx_out[4 + j : 5 + j] = delta
        if e == 1:
            ostage[0, p] = o1[p * 128 : (p + 1) * 128].astype(BF).T
            out_start(0, p)

    sx_copy = remote(sx_out, sx_in, sxs.at[0], sxr.at[0], far)

    @pl.when(late == 1)
    def _():
        sx_copy.start()

    s_start()

    def scaled(x, c_low, c_high):
        return (x.astype(F32) * jnp.where(iota(x.shape, 0) < HD, c_low, c_high)).astype(BF).T

    def backward_one(p):
        cs = (cd1[2 * p : 2 * p + 1], cd1[2 * p + 1 : 2 * p + 2])
        gc, qc = scaled(xt[G, p], *cs), scaled(xt[Q, p], *cs)
        gcs = [half_lanes(gc, e) for e in (0, 1)]
        qcs = [half_lanes(qc, e) for e in (0, 1)]
        for kb in range(NB):
            dv[p, kb * B : (kb + 1) * B] = dot(one_tail(2 * p, kb), gcs[0][kb * B :]) + dot(
                one_tail(2 * p + 1, kb), gcs[1][kb * B :]
            )
        for i in range(NB):
            n = (i + 1) * B
            for e in (0, 1):
                hh = 2 * p + e
                dp = dot(xin[V, p, :n], half_rows(xt[G, p, :, i * B : n], e))
                delta = cd1[8 + hh : 9 + hh, i * B : n]
                parts = []
                for kb in range(i + 1):
                    x = one_block(hh, kb, i)[...].astype(F32)
                    x = (x * (dp[kb * B : (kb + 1) * B] - delta)).astype(BF)
                    one_block(hh, kb, i)[...] = x
                    parts.append(x)
                dqt[hh * HD : (hh + 1) * HD, i * B : n] = dot(
                    xt[K, p, e * HD : (e + 1) * HD, :n], join(parts)
                ) * (cs[e][:, i * B : n] * 0.125)
        for kb in range(NB):
            dk[p, kb * B : (kb + 1) * B] = dot(one_tail(2 * p, kb), qcs[0][kb * B :]) + dot(
                one_tail(2 * p + 1, kb), qcs[1][kb * B :]
            )

    backward_one(0)

    @pl.when(late == 1)
    def _():
        sx_copy.wait_send()

    @pl.when(late == 0)
    def _():
        cross_wait(1, 0)
        for slot in (4, 5):
            xt[G, slot] = xin[G, slot].T
        sx_copy.wait_recv()

    def xdq_copy(p):
        at = pl.ds(p * 128, 128)
        return remote(xdq.at[0, at], xdq.at[1, at], xds.at[4 + p], xdr.at[4 + p], far)

    def xdkv_copy(n, p):
        i = n * 2 + p
        return remote(xdkv.at[0, n, p], xdkv.at[1, n, p], xds.at[i], xdr.at[i], far)

    for p in (0, 1):
        kv, qg = kv_slot + p, qg_slot + p
        cs = [sx_in[2 * p + e : 2 * p + e + 1] / stx[4 + 2 * p + e : 5 + 2 * p + e] for e in (0, 1)]
        gc, qc = scaled(xt[G, qg], *cs), scaled(xt[Q, qg], *cs)
        xdkv[0, 1, p] = (dot(pc[2 * p], half_lanes(gc, 0)) + dot(pc[2 * p + 1], half_lanes(gc, 1))).astype(BF)

        @pl.when(late == 1)
        def _():
            xdkv_copy(1, p).start()

        for i in range(NB):
            at = slice(i * B, (i + 1) * B)
            for e in (0, 1):
                hh = 2 * p + e
                dp = dot(xin[V, kv], half_rows(xt[G, qg, :, at], e))
                x = (pc[hh, :, at].astype(F32) * (dp - sx_in[4 + hh : 5 + hh, at])).astype(BF)
                pc[hh, :, at] = x
                x = dot(xt[K, kv, e * HD : (e + 1) * HD, :], x) * (cs[e][:, at] * 0.125)
                xdq[0, hh * HD : (hh + 1) * HD, at] = x.astype(BF)
        xdkv[0, 0, p] = (dot(pc[2 * p], half_lanes(qc, 0)) + dot(pc[2 * p + 1], half_lanes(qc, 1))).astype(BF)

        @pl.when(late == 1)
        def _():
            xdkv_copy(0, p).start()

        @pl.when(late == 0)
        def _():
            xdq_copy(p).start()

    s_wait()
    t_stats = jnp.concatenate([srecv[i, :, MR:CR] for i in range(M)], axis=1)
    m_stats = jnp.concatenate([srecv[i, :, :MR] for i in range(M)], axis=1)
    t_c = t_stats[0:1] / stt[0:1]
    kv_top = ttkv[...].reshape(keys_n, 128)
    dp = dot(kv_top, tg_w)
    ds = (ptop[...].astype(F32) * (dp - t_stats[1:2])).astype(BF)
    t_dq = dot(ttkv_t[HD:], ds) * (t_c * 0.125)
    t_dq = pack_halves(t_dq, 16).astype(BF).T
    gc = above((tg_w[:HD].astype(F32) * t_c).astype(BF)).T
    qc = below((tq_w[HD:].astype(F32) * t_c).astype(BF)).T
    tpart[...] = (dot(ptop[...], gc) + dot(ds, qc)).astype(BF).reshape(groups, TQ, 128)

    def part_copy(s):
        to = lax.rem(group + groups - s, groups)
        return remote(tpart.at[to], trec.at[group], tps.at[s - 1], tpr.at[s - 1], at_group(to))

    def part_arrival(s):
        frm = lax.rem(group + s, groups)
        return remote(tpart.at[frm], trec.at[frm], tps.at[s - 1], tpr.at[s - 1], at_group(lax.rem(group + groups - s, groups)))

    for s in range(1, groups):
        @pl.when(group >= s)
        def _():
            part_copy(s).start()

    m_c = m_stats[0:1] / stm[1:2]
    gc = above((mg_w[:HD].astype(F32) * m_c).astype(BF)).T
    qc = below((mq_w[HD:].astype(F32) * m_c).astype(BF)).T
    m_dv = [dot(mid_tail(kb), gc[kb * B :]) for kb in range(MB)]
    for i in range(MB):
        n = (i + 1) * B
        at = slice(i * B, n)
        dp = dot(mvg[:n], mg_w[:, at])
        parts = []
        for kb in range(i + 1):
            x = mid_block(kb, i)[...].astype(F32)
            x = (x * (dp[kb * B : (kb + 1) * B] - m_stats[1:2, at])).astype(BF)
            mid_block(kb, i)[...] = x
            parts.append(x)
        dqm[:, at] = dot(mqk_t[HD:, :n], join(parts)) * (m_c[:, at] * 0.125)
    m_vk = [m_dv[kb] + dot(mid_tail(kb), qc[kb * B :]) for kb in range(MB)]
    m_vk = jnp.concatenate(m_vk, axis=0).astype(BF)
    m_dq = pack_halves(dqm[...], MR // 2).astype(BF).T
    for i in range(M):
        gret[i, :MR] = m_vk[i * MR : (i + 1) * MR]
        gret[i, CR : CR + MR // 2] = m_dq[i * (MR // 2) : (i + 1) * (MR // 2)]
        gret[i, CR + MR // 2 :] = t_dq[i * 16 : (i + 1) * 16]
    for s in range(1, groups):
        @pl.when(group >= s)
        def _():
            part_copy(s).wait_send()

        @pl.when(group + s < groups)
        def _():
            part_arrival(s).wait_recv()

    def add_part(g, x):
        return x + trec[g].astype(F32)

    x = lax.fori_loop(group + 1, groups, add_part, tpart[group].astype(F32)).astype(BF)
    for i in range(M):
        gret[i, MR:CR] = x[i * 32 : (i + 1) * 32]
    r_start()

    backward_one(1)
    backward_one(2)
    backward_one(3)

    @pl.when(late == 0)
    def _():
        xdq_copy(0).wait_send()
        xdq_copy(1).wait_send()
        for n in (0, 1):
            for p in (0, 1):
                xdkv_copy(n, p).wait_recv()

    @pl.when(late == 1)
    def _():
        xdq_copy(0).wait_recv()
        xdq_copy(1).wait_recv()
        for n in (0, 1):
            for p in (0, 1):
                xdkv_copy(n, p).wait_send()

    r_wait()
    for p in range(4):
        rows = slice(p * 128, (p + 1) * 128)

        @pl.when(late == 1)
        def _():
            dqt[rows] += xdq[p // 2, (p % 2) * 128 : (p % 2 + 1) * 128].astype(F32)

        @pl.when(late == 0)
        def _():
            dk[p] += xdkv[1 - p // 2, 0, p % 2].astype(F32)
            dv[p] += xdkv[1 - p // 2, 1, p % 2].astype(F32)

        sums = None
        for e in (0, 1):
            cut = MR // 2
            vk, yq = gback[2 * p + e, :CR], gback[2 * p + e, CR:]
            turned = swap_halves(vk).astype(BF)
            yq = (yq, swap_halves(yq).astype(BF))
            yq = jnp.concatenate([yq[e][:cut], yq[1 - e][:cut], yq[e][cut:], yq[1 - e][cut:]], axis=0)
            if e == 0:
                y = (half_lanes(vk, 0), half_lanes(turned, 0), half_lanes(yq, 0))
            else:
                y = (half_lanes(turned, 1), half_lanes(vk, 1), half_lanes(yq, 1))
            t = dot(ehot_t[2 * p + e], jnp.concatenate(y, axis=1))
            sums = t if sums is None else sums + t
        ostage[1, p] = (dqt[rows].T + sums[:, 256:]).astype(BF)
        ostage[2, p] = (dk[p] + sums[:, 128:256]).astype(BF)
        ostage[3, p] = (dv[p] + sums[:, :128]).astype(BF)
        for a in (1, 2, 3):
            out_start(a, p)

    for a in range(4):
        for p in range(4):
            out_local(a, p).wait()
            out_copy(a, p).wait_send()
            out_arrival(a, p).wait_recv()


def hand_over(*refs):
    sources, results, (held, in_sem, out_sem) = refs[:4], refs[4:8], refs[8:]
    reads = [pltpu.make_async_copy(sources[i], held.at[i], in_sem.at[i]) for i in range(4)]
    writes = [pltpu.make_async_copy(held.at[i], results[i], out_sem.at[i]) for i in range(4)]
    for copy in reads:
        copy.start()
    for read, write in zip(reads, writes):
        read.wait()
        write.start()
    for copy in writes:
        copy.wait()


def solution(mesh):
    C = mesh.shape["ctx"]

    def shards(queries, keys, values, grad_out, offset_mid, head_top_offsets):
        T, W = queries.shape
        N = 2 * T
        CR = N // MIDDLE + 32
        R = 8 * (N // MIDDLE)
        TK = C // MIDDLE * 256
        shape = jax.ShapeDtypeStruct((T, W), BF)
        hbm = pl.BlockSpec(memory_space=pl.ANY)
        smem = pl.BlockSpec(memory_space=pltpu.SMEM)
        vm = pltpu.VMEM
        dma = pltpu.SemaphoreType.DMA
        scratch = [
            vm((8, 128), jnp.int32),
            vm((4, 8, 128), jnp.int32),
            vm((4, 6, N, 128), BF),
            vm((4, 6, 128, N), BF),
            vm((8, 2 * B, N), BF),
            vm((4, N, N), BF),
            vm((R // 2, R + B), BF),
            vm((TK, 256), BF),
            vm((8, CR, N), BF),
            vm((8, N, CR), BF),
            vm((8, CR, 256), BF),
            vm((8, CR, 256), BF),
            vm((R, 128), BF),
            vm((R, 128), BF),
            vm((128, R), BF),
            vm((128, R), BF),
            vm((128, R), BF),
            vm((128, R), BF),
            vm((256, 128), BF),
            vm((256, 128), BF),
            vm((C // MIDDLE, 256, 128), BF),
            vm((128, TK), BF),
            vm((512, N), F32),
            vm((256, N), F32),
            vm((16, N), F32),
            vm((8, N), F32),
            vm((8, R), F32),
            vm((8, 256), F32),
            vm((16, N), F32),
            vm((2, 2, 144, N), BF),
            vm((8, N), F32),
            vm((8, N), F32),
            vm((128, R), F32),
            vm((8, CR, 128), BF),
            vm((8, CR, 128), BF),
            vm((8, 8, 256), F32),
            vm((8, 8, 256), F32),
            vm((512, N), F32),
            vm((4, N, 128), F32),
            vm((4, N, 128), F32),
            vm((2, 256, N), BF),
            vm((2, 2, 2, N, 128), BF),
            vm((HD, R), F32),
            vm((8, CR + CR // 2, 128), BF),
            vm((8, CR + CR // 2, 128), BF),
            vm((C // MIDDLE, 256, 128), BF),
            vm((C // MIDDLE, 256, 128), BF),
            vm((4, 4, N, 128), BF),
            dma((3,)), dma((3,)), dma((16,)), dma((16,)), dma((16,)),
            dma((8,)), dma((8,)), dma((7,)), dma((7,)), dma((7,)), dma((7,)),
            dma((7,)), dma((7,)), dma((2,)), dma((2,)), dma((7,)), dma((7,)),
            dma((1,)), dma((1,)), dma((7,)), dma((7,)), dma((7,)), dma((7,)),
            dma((6,)), dma((6,)), dma((16,)), dma((16,)), dma((16,)),
        ]
        results = pl.pallas_call(
            functools.partial(kernel, C, T),
            out_shape=[shape] * 4,
            in_specs=[smem, smem, hbm, hbm, hbm, hbm],
            out_specs=[hbm] * 4,
            scratch_shapes=scratch,
            compiler_params=pltpu.CompilerParams(
                collective_id=0, has_side_effects=True, vmem_limit_bytes=62 << 20
            ),
            name="attention",
        )(offset_mid, head_top_offsets, queries, keys, values, grad_out)
        return pl.pallas_call(
            hand_over,
            out_shape=[shape] * 4,
            in_specs=[hbm] * 4,
            out_specs=[hbm] * 4,
            scratch_shapes=[vm((4, T, W), BF), dma((4,)), dma((4,))],
            compiler_params=pltpu.CompilerParams(vmem_limit_bytes=62 << 20),
            name="hand_over",
        )(*results)

    rows = P(("ctx", "head"), None)
    return jax.shard_map(
        shards,
        mesh=mesh,
        in_specs=(rows, rows, rows, rows, P("head"), P("head")),
        out_specs=(rows,) * 4,
        check_vma=False,
    )
```
